512 devices in a mesh: fsdp: 16 (over x, z_hi, core), tok: 32 (over z_lo, y).
Axes of the slice: x: 4, y: 8, z: 8 (z_hi: 2, z_lo: 4; z = z_hi * 4 + z_lo), core: 2. Of those that a mesh axis runs over, the one named last changes fastest.
Arguments:
- queries: bfloat16 [16, 4096, 3072], P('fsdp', 'tok'), may hold values from -6 to 6
- keys: bfloat16 [16, 4096, 3072], P('fsdp', 'tok'), may hold values from -6 to 6
- values: bfloat16 [16, 4096, 3072], P('fsdp', 'tok'), may hold values from -6 to 6
- readout: bfloat16 [3072, 1000], P('fsdp'), may hold values from -12 to 12
- global_block: int32 [16], P('fsdp'), may hold values from 0 to 31
- q_gain: float32 [3072], replicated, may hold values from 0.5 to 5
- k_gain: float32 [3072], replicated, may hold values from 0.5 to 5
Outputs:
- entropy: float32 [], replicated
- q_grad: float32 [3072], replicated
- k_grad: float32 [3072], replicated
The draws below stay inside these ranges and needn't reach their ends.
All inputs are finite; a program needn't handle non-finite values.
Results may differ from the reference program's by a relative error of at most 0.02.
The reference program's roundings to bfloat16 on the way (of `attention`) count: a program that leaves them out, or rounds other values in their place, can miss the bound.
Values may be sent and summed in bfloat16 or wider, within the bound.
A program may use at most 64 MiB of HBM per device.

```python
import jax
import jax.numpy as jnp
from jax import lax

HEADS = 24
HEAD = 128
CLASSES = 1000
ROW = 64
GBLK = 128
TOK_DEV = 128
VIEWS = 16
TOKENS_VIEW = 4096
NBLK = 32
N_TOK = 32


def shared_keys(key):
    return jax.random.truncated_normal(jax.random.fold_in(key, 7), -6.0, 6.0, (VIEWS, TOKENS_VIEW, HEADS * HEAD), jnp.float32)


def draw_keys(key, part):
    return shared_keys(key).astype(jnp.bfloat16)


def draw_queries(key, part):
    fresh = jax.random.truncated_normal(jax.random.fold_in(key, 11), -6.0, 6.0, (VIEWS, TOKENS_VIEW, HEADS * HEAD), jnp.float32)
    return fresh.astype(jnp.bfloat16)


def draw_q_gain(key, part):
    uniform_part = jax.random.uniform(jax.random.fold_in(key, 13), (HEADS * HEAD,), jnp.float32)
    return 0.5 * jnp.power(4.0, uniform_part)


def draw_k_gain(key, part):
    uniform_part = jax.random.uniform(jax.random.fold_in(key, 17), (HEADS * HEAD,), jnp.float32)
    return 0.5 * jnp.power(4.0, uniform_part)


def touch_ends(array, own_key, low, high):
    shape = array.shape
    place = [jax.random.randint(jax.random.fold_in(own_key, axis), (), 0, shape[axis]) for axis in range(len(shape))]
    array = array.at[tuple(place)].set(low)
    longest = shape.index(max(shape))
    place[longest] = (place[longest] + 1) % shape[longest]
    return array.at[tuple(place)].set(high)


def level_of(stream_key, shape, split, smallest, top_value):
    def one(position, blocks):
        draws = jax.random.uniform(jax.random.fold_in(jax.random.fold_in(stream_key, 6), position), (blocks,), jnp.float32, smallest / len(split), top_value / len(split))
        return jnp.repeat(jnp.exp(draws), shape[position] // blocks).reshape((-1,) + (1,) * (len(shape) - position - 1))

    level = one(*split[0])
    for cut in split[1:]:
        level = level * one(*cut)
    return level


def bell_draw(key, extent, deviation, limit, cuts=(), held_as=jnp.bfloat16):
    values = deviation * jax.random.normal(key, extent, jnp.float32)
    if cuts:
        values = values * level_of(key, extent, cuts, -0.22, 0.18)
    return jnp.clip(values, -limit, limit).astype(held_as)


def setup_inputs(seed: int = 0) -> dict:
    arg_keys = jax.random.split(jax.random.key(seed), 8)
    return {
        "queries": draw_queries(jax.random.fold_in(arg_keys[7], 71), 0),
        "keys": draw_keys(jax.random.fold_in(arg_keys[7], 71), 0),
        "values": bell_draw(arg_keys[2], (VIEWS, TOKENS_VIEW, HEADS * HEAD), 1.0, 6.0, ((0, 16), (1, 32))),
        "readout": bell_draw(arg_keys[3], (HEADS * HEAD, CLASSES), 2.0, 12.0, ((0, 16),)),
        "global_block": touch_ends(jax.random.randint(arg_keys[4], (VIEWS,), 0, NBLK), jax.random.fold_in(arg_keys[4], 1), 0, NBLK - 1).astype(jnp.int32),
        "q_gain": draw_q_gain(jax.random.fold_in(arg_keys[7], 71), 0),
        "k_gain": draw_k_gain(jax.random.fold_in(arg_keys[7], 71), 0),
    }


def normalize(entries, gain):
    entries = entries.astype(jnp.float32)
    average = lax.optimization_barrier(jnp.mean(entries, -1, keepdims=True))
    centred = entries - average
    variance = lax.optimization_barrier(jnp.mean(centred * centred, -1, keepdims=True))
    return (centred * lax.rsqrt(variance + 1e-06) * gain).astype(jnp.bfloat16)

def group_total(query_part, key_part, value_part, usable, gain_query, gain_key):
    query_norm = normalize(query_part, gain_query)
    key_norm = normalize(key_part, gain_key)
    scores = jnp.einsum('qhd,khd->hqk', query_norm, key_norm, preferred_element_type=jnp.float32) * HEAD ** (-0.5)
    scores = jnp.where(usable[None, None, :], scores, -1e+30)
    row_max = lax.optimization_barrier(jnp.max(scores, -1, keepdims=True))
    exponent = jnp.exp(scores - row_max)
    row_total = lax.optimization_barrier(jnp.sum(exponent, -1, keepdims=True))
    attention = (exponent / row_total).astype(jnp.bfloat16)
    return jnp.einsum('hqk,khd->hd', attention, value_part, preferred_element_type=jnp.float32)

def attend_sum(query_rows, context, usable, gain_query, gain_key, group_size):
    head_count = gain_query.shape[0] // HEAD
    query_heads = query_rows.reshape(query_rows.shape[0], head_count, HEAD)
    key_heads = context[0].reshape(context.shape[1], head_count, HEAD)
    value_heads = context[1].reshape(context.shape[1], head_count, HEAD)
    query_gains = gain_query.reshape(head_count, HEAD)
    key_gains = gain_key.reshape(head_count, HEAD)
    if group_size == head_count:
        return group_total(query_heads, key_heads, value_heads, usable, query_gains, key_gains).reshape(-1)
    checked = jax.checkpoint(group_total)

    def per_group(group_index):
        first_head = (group_index * group_size).astype(jnp.int32)
        return checked(lax.dynamic_slice_in_dim(query_heads, first_head, group_size, 1), lax.dynamic_slice_in_dim(key_heads, first_head, group_size, 1), lax.dynamic_slice_in_dim(value_heads, first_head, group_size, 1), usable, lax.dynamic_slice_in_dim(query_gains, first_head, group_size, 0), lax.dynamic_slice_in_dim(key_gains, first_head, group_size, 0))
    return lax.map(per_group, jnp.arange(head_count // group_size, dtype=jnp.int32)).reshape(-1)

def reference(queries, keys, values, readout, global_block, q_gain, k_gain):

    def loss_of(gain_query, gain_key):

        def per_view(view_index):
            query_view = lax.dynamic_index_in_dim(queries, view_index, 0, False)
            key_view = lax.dynamic_index_in_dim(keys, view_index, 0, False)
            value_view = lax.dynamic_index_in_dim(values, view_index, 0, False)
            key_value = jnp.stack([key_view, value_view])
            padded = jnp.pad(key_value, ((0, 0), (ROW, ROW), (0, 0)))
            global_id = lax.dynamic_index_in_dim(global_block, view_index, 0, False).astype(jnp.int32)
            shared = lax.dynamic_slice_in_dim(key_value, (global_id * GBLK).astype(jnp.int32), GBLK, 1)

            def per_band(band_index):
                first_row = (band_index * TOK_DEV).astype(jnp.int32)
                own_rows = lax.dynamic_slice_in_dim(key_value, first_row, TOK_DEV, 1)
                lower_rows = lax.dynamic_slice_in_dim(padded, first_row, ROW, 1)
                upper_rows = lax.dynamic_slice_in_dim(padded, (first_row + ROW + TOK_DEV).astype(jnp.int32), ROW, 1)
                context = jnp.concatenate([own_rows, lower_rows, upper_rows, shared], axis=1)
                usable = jnp.concatenate([jnp.ones((TOK_DEV,), bool), jnp.full((ROW,), band_index > 0), jnp.full((ROW,), band_index < N_TOK - 1), jnp.ones((GBLK,), bool)])
                query_rows = lax.dynamic_slice_in_dim(query_view, first_row, TOK_DEV, 0)
                return attend_sum(query_rows, context, usable, gain_query, gain_key, HEADS)
            return lax.optimization_barrier(jnp.sum(lax.map(jax.checkpoint(per_band), jnp.arange(N_TOK, dtype=jnp.int32)), 0))
        sums = lax.map(jax.checkpoint(per_view), jnp.arange(VIEWS, dtype=jnp.int32))
        pooled = sums / TOKENS_VIEW
        logits = jnp.dot(pooled, readout.astype(jnp.float32), precision=lax.Precision.HIGHEST)
        view_probs = jax.nn.softmax(logits, -1)
        mean_probs = lax.optimization_barrier(jnp.mean(view_probs, 0))
        return -jnp.sum(mean_probs * jnp.log(mean_probs))
    entropy, gradients = jax.value_and_grad(loss_of, argnums=(0, 1))(q_gain, k_gain)
    return (entropy, gradients[0], gradients[1])
```

```python
import functools

import jax
import jax.numpy as jnp
from jax import lax
from jax.experimental import pallas as pl
from jax.experimental.pallas import tpu as pltpu
from jax.sharding import PartitionSpec as P

HEAD = 128
ROW = 64
BAND = 128
CLASSES = 1000
PAD = 1024
WIN = BAND + 2 * ROW
SEEN = WIN + BAND
Y = 8
MESH = pl.DeviceIdType.MESH
F32 = jnp.float32
BF16 = jnp.bfloat16
NT = (((1,), (1,)), ((), ()))
NN = (((1,), (0,)), ((), ()))
TN = (((0,), (0,)), ((), ()))
SCALE = HEAD**-0.5


def dot(a, b, dims):
    return lax.dot_general(a, b, dims, preferred_element_type=F32)


def normalize(x, gain):
    x = x.astype(F32)
    x = x - jnp.mean(x, -1, keepdims=True)
    var = jnp.mean(x * x, -1, keepdims=True)
    return (x * lax.rsqrt(var + 1e-06) * gain).astype(BF16)


def split3(x):
    x = jnp.broadcast_to(x, (16, x.shape[1]))
    high = x.astype(BF16).astype(F32)
    rest = x - high
    mid = rest.astype(BF16).astype(F32)
    low = rest - mid
    row = lax.broadcasted_iota(jnp.int32, x.shape, 0)
    out = jnp.where(row == 0, high, jnp.where(row == 1, mid, jnp.where(row == 2, low, 0.0)))
    return out.astype(BF16)


def row_dot(x, b, dims):
    return jnp.sum(dot(split3(x), b, dims), 0, keepdims=True)


def kernel(
    ny, nz, nf, hc, tokens,
    gid_ref, q_ref, k_ref, v_ref, r_ref, qg_ref, kg_ref,
    ent_ref, w_out,
    kpad, vpad, qbuf, knpad, kng, zk, zv, rraw, rpad, att, qn_s, w_s, e_acc, eg_acc, e_bf, eg_bf,
    lbuf, pbuf, wbuf, tbuf,
    ks, kr, vs, vr, qs, qr, local, zks, zkr, zvs, zvr, hks, hkr, hvs, hvr,
    rs, rr, fs, fr, lsem, lrem, psem, prem, wsem, wrem, tsem, trem,
):
    nt = nz * ny
    f, t = lax.axis_index("fsdp"), lax.axis_index("tok")
    z, y = t // ny, t % ny
    core = f % 2
    width = hc * HEAD
    rows = ny * BAND
    shard = r_ref.shape[0]

    def copy(src, dst, ssem, rsem, dev):
        return pltpu.make_async_remote_copy(
            src_ref=src, dst_ref=dst, send_sem=ssem, recv_sem=rsem, device_id=dev, device_id_type=MESH
        )

    def chunk(c):
        return pl.ds(pl.multiple_of(c * width, HEAD), width)

    def band_rows(b):
        return pl.ds(pl.multiple_of(ROW + b * BAND, ROW), BAND)

    own_k = pltpu.make_async_copy(k_ref.at[0, :, chunk(y)], kpad.at[band_rows(y)], local.at[0])
    own_v = pltpu.make_async_copy(v_ref.at[0, :, chunk(y)], vpad.at[band_rows(y)], local.at[1])
    own_q = pltpu.make_async_copy(q_ref.at[0, :, chunk(y)], qbuf.at[y], local.at[2])
    own_k.start()
    own_v.start()
    own_q.start()

    barrier = pltpu.get_barrier_semaphore()

    def greet_t(d, carry):
        pl.semaphore_signal(barrier, inc=1, device_id=(f, (t + d) % nt), device_id_type=MESH)
        return carry

    def greet_f(d, carry):
        pl.semaphore_signal(barrier, inc=1, device_id=((f + d) % nf, t), device_id_type=MESH)
        return carry

    lax.fori_loop(1, nt, greet_t, 0)
    lax.fori_loop(1, nf, greet_f, 0)
    pl.semaphore_wait(barrier, nt - 1 + nf - 1)

    order = [0]
    for d in range(1, ny // 2 + 1):
        order.append(d)
        if ny - d != d:
            order.append(ny - d)

    def y_dev(d):
        return (f, z * ny + (y + d) % ny)

    def k_copy(d):
        p = (y + d) % ny
        return copy(k_ref.at[0, :, chunk(p)], kpad.at[band_rows(y)], ks.at[d], kr.at[d], y_dev(d))

    def v_copy(d):
        p = (y + d) % ny
        return copy(v_ref.at[0, :, chunk(p)], vpad.at[band_rows(y)], vs.at[d], vr.at[d], y_dev(d))

    def q_copy(d):
        p = (y + d) % ny
        return copy(q_ref.at[0, :, chunk(p)], qbuf.at[y], qs.at[d], qr.at[d], y_dev(d))

    far_first = order[:0:-1]
    for d in far_first:
        k_copy(d).start()

    mine = pl.ds(pl.multiple_of(core * shard, 64), shard)
    has_rows = f // 2 == y

    def r_copy(d):
        return copy(r_ref, rraw.at[mine], rs.at[d], rr.at[0], ((f + 2 * d) % nf, t))

    def r_local():
        return pltpu.make_async_copy(r_ref, rraw.at[mine], local.at[3])

    @pl.when(has_rows)
    def _():
        for d in range(1, nf // 2):
            r_copy(d).start()
        r_local().start()

    for d in far_first:
        k_copy(d).wait_send()
    for d in far_first:
        v_copy(d).start()

    own_k.wait()
    for d in far_first:
        k_copy(d).wait_recv()
    gid = gid_ref[0]
    gid_y, gid_z = lax.rem(gid, ny), lax.div(gid, ny)

    def pick(parts, want):
        out = None
        for i, part in enumerate(parts):
            part = part.astype(F32) * jnp.where(want == i, 1.0, 0.0)
            out = part if out is None else out + part
        return out.astype(BF16)

    def pick_row(pad):
        return pick([pad[ROW + b * BAND : ROW + (b + 1) * BAND, :] for b in range(ny)], gid_y)

    def z_dev(d):
        return (f, ((z + d) % nz) * ny + y)

    def z_copy(buf, ssem, rsem, d):
        return copy(buf.at[z], buf.at[z], ssem.at[d], rsem.at[d], z_dev(d))

    def end_copies(pad, ssem, rsem):
        up = copy(pad.at[pl.ds(rows, ROW)], pad.at[pl.ds(0, ROW)], ssem.at[0], rsem.at[0], z_dev(1))
        down = copy(pad.at[pl.ds(ROW, ROW)], pad.at[pl.ds(ROW + rows, ROW)], ssem.at[1], rsem.at[1], z_dev(nz - 1))
        return up, down

    zk[z] = pick_row(kpad)
    for d in range(1, nz):
        z_copy(zk, zks, zkr, d).start()
    for c in end_copies(kpad, hks, hkr):
        c.start()

    q_gain = [qg_ref[pl.ds(y * hc + h, 1), :] for h in range(hc)]
    k_gain = [kg_ref[pl.ds(y * hc + h, 1), :] for h in range(hc)]
    knpad[:, :, HEAD:] = jnp.ones((hc, rows + 2 * ROW, HEAD), BF16)
    kng[:, :, HEAD:] = jnp.ones((hc, BAND, HEAD), BF16)

    def norm_rows(at, size):
        for h in range(hc):
            knpad[h, at, :HEAD] = normalize(kpad[at, h * HEAD : (h + 1) * HEAD], k_gain[h])

    def norm_band(b, carry):
        norm_rows(band_rows(b), BAND)
        return carry

    lax.fori_loop(0, ny, norm_band, 0)

    for d in far_first:
        v_copy(d).wait_send()
    for d in far_first:
        q_copy(d).start()

    for d in range(1, nz):
        z_copy(zk, zks, zkr, d).wait_recv()
    for c in end_copies(kpad, hks, hkr):
        c.wait_recv()
    norm_rows(pl.ds(0, ROW), ROW)
    norm_rows(pl.ds(ROW + rows, ROW), ROW)
    kg_raw = pick([zk[i] for i in range(nz)], gid_z)
    for h in range(hc):
        kng[h, :, :HEAD] = normalize(kg_raw[:, h * HEAD : (h + 1) * HEAD], k_gain[h])

    own_v.wait()
    for d in far_first:
        v_copy(d).wait_recv()
    zv[z] = pick_row(vpad)
    for d in range(1, nz):
        z_copy(zv, zvs, zvr, d).start()
    for c in end_copies(vpad, hvs, hvr):
        c.start()

    @pl.when(has_rows)
    def _():
        r_local().wait()

    @pl.when(jnp.logical_not(has_rows))
    def _():
        r_copy(1).wait_recv()

    def twin_copy(at):
        return copy(rraw.at[at], rraw.at[at], fs, fr, (f + 1 - 2 * core, t))

    twin_copy(mine).start()

    ones16 = jnp.ones((16, BAND), BF16)
    lane = lax.broadcasted_iota(jnp.int32, (BAND, WIN), 1)

    def band(b):
        low = jnp.where((z == 0) & (b == 0), ROW, 0)
        high = jnp.where((z == nz - 1) & (b == ny - 1), ROW + BAND, WIN)
        usable = (lane >= low) & (lane < high)
        window = pl.ds(pl.multiple_of(b * BAND, BAND), WIN)
        for h in range(hc):
            qn = normalize(qbuf[b, :, h * HEAD : (h + 1) * HEAD], q_gain[h])
            qn_s[b, h] = qn
            near = dot(qn, knpad[h, window, :HEAD], NT) * SCALE
            far = dot(qn, kng[h, :, :HEAD], NT) * SCALE
            near = jnp.where(usable, near, -1e30)
            top = jnp.maximum(jnp.max(near, -1, keepdims=True), jnp.max(far, -1, keepdims=True))
            near = jnp.exp(near - top)
            far = jnp.exp(far - top)
            total = jnp.sum(near, -1, keepdims=True) + jnp.sum(far, -1, keepdims=True)
            inv = 1.0 / total
            near = (near * inv).astype(BF16)
            far = (far * inv).astype(BF16)
            att[b, h, :, :WIN] = near
            att[b, h, :, WIN:] = far
            w_s[b, h, :, :WIN] = dot(ones16, near, NN)[:8]
            w_s[b, h, :, WIN:] = dot(ones16, far, NN)[:8]

    own_q.wait()
    for d in order:
        if d:
            q_copy(ny - d).wait_recv()
        band((y + d) % ny)

    for d in range(1, nz):
        z_copy(zv, zvs, zvr, d).wait_recv()
    for c in end_copies(vpad, hvs, hvr):
        c.wait_recv()
    other = pl.ds(pl.multiple_of((1 - core) * shard, 64), shard)
    twin_copy(other).wait_recv()
    rpad[:, CLASSES // HEAD * HEAD :] = jnp.zeros((width, PAD - CLASSES // HEAD * HEAD), BF16)
    rpad[:, :CLASSES] = rraw[...]

    vg = pick([zv[i] for i in range(nz)], gid_z)
    pooled = []
    for h in range(hc):
        parts = [jnp.zeros((1, HEAD), F32) for _ in range(ny + 1)]
        far = jnp.zeros((1, HEAD), F32)
        for b in range(ny):
            parts[b] = parts[b] + w_s[b, h, 0:1, :HEAD]
            parts[b + 1] = parts[b + 1] + w_s[b, h, 0:1, HEAD:WIN]
            far = far + w_s[b, h, 0:1, WIN:]
        cols = slice(h * HEAD, (h + 1) * HEAD)
        pooled.append(row_dot(jnp.concatenate(parts, 1), vpad[:, cols], NN) + row_dot(far, vg[:, cols], NN))
    pooled = jnp.concatenate(pooled, 1) * (1.0 / tokens)
    logits = row_dot(pooled, rpad[...], NN)
    for i in range(8):
        lbuf[t, i : i + 1, :] = logits[:, i * HEAD : (i + 1) * HEAD]

    def exchange(buf, n, me, dev, ssem, rsem):
        def one(d):
            return copy(buf.at[me], buf.at[me], ssem.at[d], rsem.at[d], dev((me + d) % n))

        def start():
            def step(d, carry):
                one(d).start()
                return carry

            lax.fori_loop(1, n, step, 0)

        def wait():
            def step(d, carry):
                one(d).wait_recv()
                return carry

            lax.fori_loop(1, n, step, 0)

        def wait_sent():
            def step(d, carry):
                one(d).wait_send()
                return carry

            lax.fori_loop(1, n, step, 0)

        return start, wait, wait_sent

    def t_dev(p):
        return (f, p)

    def f_dev(p):
        return (p, t)

    def total_of(buf, n):
        out = buf[0]
        for i in range(1, n):
            out = out + buf[i]
        return out

    l_start, l_wait, l_sent = exchange(lbuf, nt, t, t_dev, lsem, lrem)
    p_start, p_wait, p_sent = exchange(pbuf, nf, f, f_dev, psem, prem)
    w_start, w_wait, w_sent = exchange(wbuf, nf, f, f_dev, wsem, wrem)
    t_start, t_wait, t_sent = exchange(tbuf, nt, t, t_dev, tsem, trem)
    l_start()

    e_acc[...] = jnp.zeros_like(e_acc)
    eg_acc[...] = jnp.zeros_like(eg_acc)

    def pulled(b, carry):
        window = pl.ds(pl.multiple_of(b * BAND, BAND), WIN)
        for h in range(hc):
            near = att[b, h, :, :WIN]
            far = att[b, h, :, WIN:]
            kn = knpad[h, window, :]
            kg = kng[h]
            mean_key = dot(near, kn, NN) + dot(far, kg, NN)
            qn = qn_s[b, h]
            qk = qn.astype(F32) * (mean_key[:, :HEAD] / mean_key[:, HEAD:])
            qk_high = qk.astype(BF16)
            qk_low = (qk - qk_high.astype(F32)).astype(BF16)
            right = jnp.concatenate([qn, qk_high, qk_low], 1)
            got = dot(near, right, TN)
            e_acc[h, window, :] += (
                kn[:, :HEAD].astype(F32) * got[:, :HEAD] - got[:, HEAD : 2 * HEAD] - got[:, 2 * HEAD :]
            )
            got = dot(far, right, TN)
            eg_acc[h] += kg[:, :HEAD].astype(F32) * got[:, :HEAD] - got[:, HEAD : 2 * HEAD] - got[:, 2 * HEAD :]
        return carry

    lax.fori_loop(0, ny // 2, pulled, 0)

    l_wait()
    logits = total_of(lbuf, nt)
    place = lax.broadcasted_iota(jnp.int32, (8, HEAD), 0) * HEAD + lax.broadcasted_iota(jnp.int32, (8, HEAD), 1)
    valid = place < CLASSES
    logits = jnp.where(valid, logits, -jnp.inf)

    def all_sum(x):
        return jnp.sum(jnp.sum(x, 0, keepdims=True), 1, keepdims=True)

    top = jnp.max(jnp.max(logits, 0, keepdims=True), 1, keepdims=True)
    probs = jnp.exp(logits - top)
    probs = probs / all_sum(probs)
    pbuf[f] = probs
    p_start()

    lax.fori_loop(ny // 2, ny, pulled, 0)
    e_bf[...] = e_acc[...].astype(BF16)
    eg_bf[...] = eg_acc[...].astype(BF16)

    p_wait()
    mean = total_of(pbuf, nf) * (1.0 / nf)
    log_mean = jnp.where(valid, jnp.log(mean), 0.0)
    entropy = -all_sum(jnp.where(valid, mean * log_mean, 0.0))
    ent_ref[...] = jnp.broadcast_to(entropy, ent_ref.shape)
    upstream = jnp.where(valid, -(log_mean + 1.0) * (1.0 / nf), 0.0)
    dlogits = probs * (upstream - all_sum(probs * upstream))
    dlogits = jnp.concatenate([dlogits[i : i + 1] for i in range(8)], 1)
    dpooled = row_dot(dlogits, rpad[...], NT) * (1.0 / tokens)
    wbuf[f] = jnp.zeros((8, HEAD), F32)
    for h in range(hc):
        cols = slice(h * HEAD, (h + 1) * HEAD)
        down = dpooled[:, cols]
        near = row_dot(down, vpad[:, cols], NT)
        far = row_dot(down, vg[:, cols], NT)
        middle = (jnp.sum(near, 1, keepdims=True) + jnp.sum(far, 1, keepdims=True)) * (1.0 / (rows + 2 * ROW + BAND))
        got = row_dot(near - middle, e_bf[h], NN) + row_dot(far - middle, eg_bf[h], NN)
        wbuf[f, h : h + 1, :] = got * SCALE
    w_start()
    w_wait()
    tbuf[t] = total_of(wbuf, nf)
    t_start()
    t_wait()
    for i in range(ny):
        got = tbuf[i]
        for j in range(1, nz):
            got = got + tbuf[j * ny + i]
        w_out[i * hc : (i + 1) * hc, :] = got[:hc]

    for d in far_first:
        q_copy(d).wait_send()
    for d in range(1, nz):
        z_copy(zk, zks, zkr, d).wait_send()
        z_copy(zv, zvs, zvr, d).wait_send()
    for c in end_copies(kpad, hks, hkr) + end_copies(vpad, hvs, hvr):
        c.wait_send()

    @pl.when(has_rows)
    def _():
        for d in range(1, nf // 2):
            r_copy(d).wait_send()

    twin_copy(mine).wait_send()
    l_sent()
    p_sent()
    w_sent()
    t_sent()


def make_body(ny):
    def body(queries, keys, values, readout, global_block, q_gain, k_gain):
        nf, nt = lax.axis_size("fsdp"), lax.axis_size("tok")
        nz = nt // ny
        heads = q_gain.shape[0] // HEAD
        hc = heads // ny
        width = hc * HEAD
        rows = ny * BAND
        padded = rows + 2 * ROW
        tokens = nt * BAND
        dma = pltpu.SemaphoreType.DMA
        vmem = pltpu.VMEM
        scratch = [
            vmem((padded, width), BF16),
            vmem((padded, width), BF16),
            vmem((ny, BAND, width), BF16),
            vmem((hc, padded, 2 * HEAD), BF16),
            vmem((hc, BAND, 2 * HEAD), BF16),
            vmem((nz, BAND, width), BF16),
            vmem((nz, BAND, width), BF16),
            vmem((width, CLASSES), BF16),
            vmem((width, PAD), BF16),
            vmem((ny, hc, BAND, SEEN), BF16),
            vmem((ny, hc, BAND, HEAD), BF16),
            vmem((ny, hc, 8, SEEN), F32),
            vmem((hc, padded, HEAD), F32),
            vmem((hc, BAND, HEAD), F32),
            vmem((hc, padded, HEAD), BF16),
            vmem((hc, BAND, HEAD), BF16),
            vmem((nt, 8, HEAD), F32),
            vmem((nf, 8, HEAD), F32),
            vmem((nf, 8, HEAD), F32),
            vmem((nt, 8, HEAD), F32),
        ]
        scratch += [dma((ny,))] * 6 + [dma((4,))] + [dma((nz,))] * 4 + [dma((2,))] * 4
        scratch += [dma((nf // 2,)), dma((1,)), dma, dma]
        scratch += [dma((nt,))] * 2 + [dma((nf,))] * 4 + [dma((nt,))] * 2
        hbm = pl.BlockSpec(memory_space=pl.ANY)
        whole = pl.BlockSpec(memory_space=pltpu.VMEM)
        entropy, total = pl.pallas_call(
            functools.partial(kernel, ny, nz, nf, hc, tokens),
            out_shape=(
                jax.ShapeDtypeStruct((8, HEAD), F32),
                jax.ShapeDtypeStruct((heads, HEAD), F32),
            ),
            in_specs=[pl.BlockSpec(memory_space=pltpu.SMEM), hbm, hbm, hbm, hbm, whole, whole],
            out_specs=(whole, whole),
            scratch_shapes=scratch,
            compiler_params=pltpu.CompilerParams(
                collective_id=0, has_side_effects=True, vmem_limit_bytes=60 * 2**20
            ),
            name="adapt",
        )(
            global_block,
            queries,
            keys,
            values,
            readout,
            q_gain.reshape(heads, HEAD),
            k_gain.reshape(heads, HEAD),
        )
        total = total.reshape(-1)
        return entropy[0, 0], total / q_gain, total / k_gain

    return body


def solution(mesh):
    in_specs = (
        P("fsdp", "tok", None),
        P("fsdp", "tok", None),
        P("fsdp", "tok", None),
        P("fsdp", None),
        P("fsdp"),
        P(),
        P(),
    )
    out_specs = (P(), P(), P())
    return jax.shard_map(make_body(Y), mesh=mesh, in_specs=in_specs, out_specs=out_specs, check_vma=False)
```

```python
import functools

import jax
import jax.numpy as jnp
from jax import lax
from jax.experimental import pallas as pl
from jax.experimental.pallas import tpu as pltpu
from jax.sharding import PartitionSpec as P

HEAD = 128
ROW = 64
BAND = 128
CLASSES = 1000
PAD = 1024
WIN = BAND + 2 * ROW
SEEN = WIN + BAND
Y = 8
MESH = pl.DeviceIdType.MESH
F32 = jnp.float32
BF16 = jnp.bfloat16
NT = (((1,), (1,)), ((), ()))
NN = (((1,), (0,)), ((), ()))
TN = (((0,), (0,)), ((), ()))
SCALE = HEAD**-0.5


def dot(a, b, dims):
    return lax.dot_general(a, b, dims, preferred_element_type=F32)


def normalize(x, gain):
    x = x.astype(F32)
    x = x - jnp.mean(x, -1, keepdims=True)
    var = jnp.mean(x * x, -1, keepdims=True)
    return (x * lax.rsqrt(var + 1e-06) * gain).astype(BF16)


def split3(x):
    x = jnp.broadcast_to(x, (16, x.shape[1]))
    high = x.astype(BF16).astype(F32)
    rest = x - high
    mid = rest.astype(BF16).astype(F32)
    low = rest - mid
    row = lax.broadcasted_iota(jnp.int32, x.shape, 0)
    out = jnp.where(row == 0, high, jnp.where(row == 1, mid, jnp.where(row == 2, low, 0.0)))
    return out.astype(BF16)


def row_dot(x, b, dims):
    return jnp.sum(dot(split3(x), b, dims), 0, keepdims=True)


def kernel(
    ny, nz, nf, hc, tokens,
    gid_hbm, q_ref, k_ref, v_ref, r_ref, qg_hbm, kg_hbm,
    ent_ref, w_out,
    gid_ref, qg_ref, kg_ref,
    kpad, vbuf, vend, qbuf, knpad, kng, zk, zv, zw, rraw, rpad, att, qn_s, w_s, e_acc, eg_acc, e_bf, pull,
    lbuf, pbuf, wbuf, tbuf,
    ks, kr, vs, vr, qs, qr, local, zks, zkr, zvs, zvr, hks, hkr, hvs, hvr, zws, zwr,
    rs, rr, fs, fr, lsem, lrem, psem, prem, wsem, wrem, tsem, trem,
):
    nt = nz * ny
    f, t = lax.axis_index("fsdp"), lax.axis_index("tok")
    z, y = t // ny, t % ny
    core = f % 2
    width = hc * HEAD
    rows = ny * BAND
    shard = r_ref.shape[0]

    def copy(src, dst, ssem, rsem, dev):
        return pltpu.make_async_remote_copy(
            src_ref=src, dst_ref=dst, send_sem=ssem, recv_sem=rsem, device_id=dev, device_id_type=MESH
        )

    def chunk(c):
        return pl.ds(pl.multiple_of(c * width, HEAD), width)

    def band_rows(b):
        return pl.ds(pl.multiple_of(ROW + b * BAND, ROW), BAND)

    own_k = pltpu.make_async_copy(k_ref.at[0, :, chunk(y)], kpad.at[band_rows(y)], local.at[0])
    own_v = pltpu.make_async_copy(v_ref.at[0, :, chunk(y)], vbuf.at[y], local.at[1])
    own_q = pltpu.make_async_copy(q_ref.at[0, :, chunk(y)], qbuf.at[y], local.at[2])
    own_k.start()
    own_v.start()
    own_q.start()

    small = [
        pltpu.make_async_copy(gid_hbm, gid_ref, local.at[4]),
        pltpu.make_async_copy(qg_hbm, qg_ref, local.at[5]),
        pltpu.make_async_copy(kg_hbm, kg_ref, local.at[6]),
    ]
    for c in small:
        c.start()

    chip = f // 2
    mirror_t = (nz - 1 - z) * ny + y

    def wrap(i, n):
        return jnp.where(i >= n, i - n, i)

    def t_dev(p):
        return (f, p)

    def f_dev(p):
        return (p, jnp.where((p // 2) % 2 == chip % 2, t, mirror_t))

    barrier = pltpu.get_barrier_semaphore()

    def greet(dev):
        pl.semaphore_signal(barrier, inc=1, device_id=dev, device_id_type=MESH)

    for d in range(1, ny):
        greet((f, z * ny + wrap(y + d, ny)))

    def greet_t(i, carry):
        far_z = wrap(z + i // ny, nz)
        greet((f, far_z * ny + i % ny))
        return carry

    def greet_f(d, carry):
        greet(f_dev(wrap(f + d, nf)))
        return carry

    lax.fori_loop(1, nf, greet_f, 0)
    lax.fori_loop(ny, nt, greet_t, 0)
    pl.semaphore_wait(barrier, nt - 1 + nf - 1)

    order = [0]
    for d in range(1, ny // 2 + 1):
        order.append(d)
        if ny - d != d:
            order.append(ny - d)

    def y_dev(d):
        return (f, z * ny + (y + d) % ny)

    def k_copy(d):
        p = (y + d) % ny
        return copy(k_ref.at[0, :, chunk(p)], kpad.at[band_rows(y)], ks.at[d], kr.at[d], y_dev(d))

    def v_copy(d):
        p = (y + d) % ny
        return copy(v_ref.at[0, :, chunk(p)], vbuf.at[y], vs.at[d], vr.at[d], y_dev(d))

    def q_copy(d):
        p = (y + d) % ny
        return copy(q_ref.at[0, :, chunk(p)], qbuf.at[y], qs.at[d], qr.at[d], y_dev(d))

    far_first = order[:0:-1]
    for d in far_first:
        k_copy(d).start()

    mine = pl.ds(pl.multiple_of(core * shard, 64), shard)
    holder = chip == y
    relay = (chip // 2 == y // 2) & (chip != y)
    leaf = chip // 2 != y // 2
    lines = range(1, nf // 4)

    def x_copy(src, d):
        return copy(src, rraw.at[mine], rs.at[d], rr.at[0], ((f + 4 * d) % nf, t))

    def mirror_copy():
        return copy(r_ref, rraw.at[mine], rs.at[0], rr.at[0], f_dev(f + 2 - 4 * (chip % 2)))

    def r_local():
        return pltpu.make_async_copy(r_ref, rraw.at[mine], local.at[3])

    @pl.when(holder)
    def _():
        mirror_copy().start()
        for d in lines:
            x_copy(r_ref, d).start()
        r_local().start()

    for d in far_first:
        k_copy(d).wait_send()
    for d in far_first:
        q_copy(d).start()

    own_k.wait()
    for d in far_first:
        k_copy(d).wait_recv()
    for c in small:
        c.wait()
    gid = gid_ref[0]
    gid_y, gid_z = lax.rem(gid, ny), lax.div(gid, ny)

    def pick(parts, want):
        out = None
        for i, part in enumerate(parts):
            part = part.astype(F32) * jnp.where(want == i, 1.0, 0.0)
            out = part if out is None else out + part
        return out.astype(BF16)

    def z_dev(d):
        return (f, ((z + d) % nz) * ny + y)

    def z_copy(buf, ssem, rsem, d):
        return copy(buf.at[z], buf.at[z], ssem.at[d], rsem.at[d], z_dev(d))

    def k_ends():
        up = copy(kpad.at[pl.ds(rows, ROW)], kpad.at[pl.ds(0, ROW)], hks.at[0], hkr.at[0], z_dev(1))
        down = copy(kpad.at[pl.ds(ROW, ROW)], kpad.at[pl.ds(ROW + rows, ROW)], hks.at[1], hkr.at[1], z_dev(nz - 1))
        return up, down

    def v_ends():
        low, high = pl.ds(0, ROW), pl.ds(ROW, ROW)
        up = copy(vbuf.at[ny - 1, high], vend.at[low], hvs.at[0], hvr.at[0], z_dev(1))
        down = copy(vbuf.at[0, low], vend.at[high], hvs.at[1], hvr.at[1], z_dev(nz - 1))
        return up, down

    zk[z] = pick([kpad[ROW + b * BAND : ROW + (b + 1) * BAND, :] for b in range(ny)], gid_y)
    for d in range(1, nz):
        z_copy(zk, zks, zkr, d).start()
    for c in k_ends():
        c.start()

    q_gain = [qg_ref[pl.ds(y * hc + h, 1), :] for h in range(hc)]
    k_gain = [kg_ref[pl.ds(y * hc + h, 1), :] for h in range(hc)]
    knpad[:, :, HEAD:] = jnp.ones((hc, rows + 2 * ROW, HEAD), BF16)
    kng[:, :, HEAD:] = jnp.ones((hc, BAND, HEAD), BF16)

    def norm_rows(at, size):
        for h in range(hc):
            knpad[h, at, :HEAD] = normalize(kpad[at, h * HEAD : (h + 1) * HEAD], k_gain[h])

    def norm_band(b, carry):
        norm_rows(band_rows(b), BAND)
        return carry

    lax.fori_loop(0, ny, norm_band, 0)

    for d in far_first:
        q_copy(d).wait_send()
    for d in far_first:
        v_copy(d).start()

    for d in range(1, nz):
        z_copy(zk, zks, zkr, d).wait_recv()
    for c in k_ends():
        c.wait_recv()
    norm_rows(pl.ds(0, ROW), ROW)
    norm_rows(pl.ds(ROW + rows, ROW), ROW)
    kg_raw = pick([zk[i] for i in range(nz)], gid_z)
    for h in range(hc):
        kng[h, :, :HEAD] = normalize(kg_raw[:, h * HEAD : (h + 1) * HEAD], k_gain[h])

    @pl.when(relay)
    def _():
        mirror_copy().wait_recv()
        for d in lines:
            x_copy(rraw.at[mine], d).start()

    ones16 = jnp.ones((16, BAND), BF16)
    lane = lax.broadcasted_iota(jnp.int32, (BAND, WIN), 1)

    def band(b):
        low = jnp.where((z == 0) & (b == 0), ROW, 0)
        high = jnp.where((z == nz - 1) & (b == ny - 1), ROW + BAND, WIN)
        usable = (lane >= low) & (lane < high)
        window = pl.ds(pl.multiple_of(b * BAND, BAND), WIN)
        for h in range(hc):
            qn = normalize(qbuf[b, :, h * HEAD : (h + 1) * HEAD], q_gain[h])
            qn_s[b, h] = qn
            near = dot(qn, knpad[h, window, :HEAD], NT) * SCALE
            far = dot(qn, kng[h, :, :HEAD], NT) * SCALE
            near = jnp.where(usable, near, -1e30)
            top = jnp.maximum(jnp.max(near, -1, keepdims=True), jnp.max(far, -1, keepdims=True))
            near = jnp.exp(near - top)
            far = jnp.exp(far - top)
            total = jnp.sum(near, -1, keepdims=True) + jnp.sum(far, -1, keepdims=True)
            inv = 1.0 / total
            near = (near * inv).astype(BF16)
            far = (far * inv).astype(BF16)
            att[b, h, :, :WIN] = near
            att[b, h, :, WIN:] = far
            w_s[b, h, :, :WIN] = dot(ones16, near, NN)[:8]
            w_s[b, h, :, WIN:] = dot(ones16, far, NN)[:8]

    own_q.wait()
    for d in order:
        if d:
            q_copy(ny - d).wait_recv()
        band((y + d) % ny)

    half = lax.broadcasted_iota(jnp.int32, (1, HEAD), 1) < ROW
    given = []
    zw[z] = jnp.zeros((8, HEAD), F32)
    for h in range(hc):
        parts = [jnp.zeros((1, HEAD), F32) for _ in range(ny + 1)]
        far = jnp.zeros((1, HEAD), F32)
        for b in range(ny):
            parts[b] = parts[b] + w_s[b, h, 0:1, :HEAD]
            parts[b + 1] = parts[b + 1] + w_s[b, h, 0:1, HEAD:WIN]
            far = far + w_s[b, h, 0:1, WIN:]
        given.append(parts)
        zw[z, h : h + 1, :] = far
        zw[z, hc + h : hc + h + 1, :] = jnp.where(half, parts[0], parts[ny])
    for d in range(1, nz):
        z_copy(zw, zws, zwr, d).start()

    @pl.when(holder)
    def _():
        r_local().wait()

    if nf > 4:

        @pl.when(leaf)
        def _():
            mirror_copy().wait_recv()

    def twin_copy(at):
        return copy(rraw.at[at], rraw.at[at], fs, fr, (f + 1 - 2 * core, t))

    twin_copy(mine).start()

    e_acc[...] = jnp.zeros_like(e_acc)
    eg_acc[...] = jnp.zeros_like(eg_acc)

    def pulled(b, carry):
        window = pl.ds(pl.multiple_of(b * BAND, BAND), WIN)
        for h in range(hc):
            near = att[b, h, :, :WIN]
            far = att[b, h, :, WIN:]
            kn = knpad[h, window, :]
            kg = kng[h]
            mean_key = dot(near, kn, NN) + dot(far, kg, NN)
            qn = qn_s[b, h]
            qk = qn.astype(F32) * (mean_key[:, :HEAD] / mean_key[:, HEAD:])
            qk_high = qk.astype(BF16)
            qk_low = (qk - qk_high.astype(F32)).astype(BF16)
            right = jnp.concatenate([qn, qk_high, qk_low], 1)
            got = dot(near, right, TN)
            e_acc[h, window, :] += (
                kn[:, :HEAD].astype(F32) * got[:, :HEAD] - got[:, HEAD : 2 * HEAD] - got[:, 2 * HEAD :]
            )
            got = dot(far, right, TN)
            eg_acc[h] += kg[:, :HEAD].astype(F32) * got[:, :HEAD] - got[:, HEAD : 2 * HEAD] - got[:, 2 * HEAD :]
        return carry

    def pull_bands(first, last):
        lax.fori_loop(min(first, ny), min(last, ny), pulled, 0)

    pull_bands(0, 2)

    other = pl.ds(pl.multiple_of((1 - core) * shard, 64), shard)
    twin_copy(other).wait_recv()
    rpad[:, CLASSES // HEAD * HEAD :] = jnp.zeros((width, PAD - CLASSES // HEAD * HEAD), BF16)
    rpad[:, :CLASSES] = rraw[...]

    for d in range(1, nz):
        z_copy(zw, zws, zwr, d).wait_recv()
    below = zw[lax.rem(z + nz - 1, nz)]
    above = zw[lax.rem(z + 1, nz)]
    all_far = zw[0]
    for i in range(1, nz):
        all_far = all_far + zw[i]
    weights = []
    for h in range(hc):
        parts = given[h]
        parts[0] = parts[0] + below[hc + h : hc + h + 1]
        parts[ny] = parts[ny] + above[hc + h : hc + h + 1]
        own = []
        for b in range(ny):
            tile = jnp.concatenate([parts[b][:, ROW:], parts[b + 1][:, :ROW]], 1)
            own.append(tile + all_far[h : h + 1] * jnp.where(gid == z * ny + b, 1.0, 0.0))
        weights.append(split3(jnp.concatenate(own, 1)))

    def v_head(h):
        return vbuf[:, :, h * HEAD : (h + 1) * HEAD].reshape(rows, HEAD)

    own_v.wait()
    for d in far_first:
        v_copy(d).wait_recv()
    pooled = [jnp.sum(dot(weights[h], v_head(h), NN), 0, keepdims=True) for h in range(hc)]
    pooled = jnp.concatenate(pooled, 1) * (1.0 / tokens)
    logits = row_dot(pooled, rpad[...], NN)
    for i in range(8):
        lbuf[t, i : i + 1, :] = logits[:, i * HEAD : (i + 1) * HEAD]

    def exchange(buf, n, me, dev, ssem, rsem):
        def one(d):
            return copy(buf.at[me], buf.at[me], ssem.at[d], rsem.at[d], dev(jnp.where(me + d >= n, me + d - n, me + d)))

        def start():
            def step(d, carry):
                one(d).start()
                return carry

            lax.fori_loop(1, n, step, 0)

        def wait():
            def step(d, carry):
                one(d).wait_recv()
                return carry

            lax.fori_loop(1, n, step, 0)

        def wait_sent():
            def step(d, carry):
                one(d).wait_send()
                return carry

            lax.fori_loop(1, n, step, 0)

        return start, wait, wait_sent

    def total_of(buf, n):
        out = buf[0]
        for i in range(1, n):
            out = out + buf[i]
        return out

    l_start, l_wait, l_sent = exchange(lbuf, nt, t, t_dev, lsem, lrem)
    p_start, p_wait, p_sent = exchange(pbuf, nf, f, f_dev, psem, prem)
    w_start, w_wait, w_sent = exchange(wbuf, nf, f, f_dev, wsem, wrem)
    t_start, t_wait, t_sent = exchange(tbuf, nt, t, t_dev, tsem, trem)
    l_start()

    for c in v_ends():
        c.start()
    zv[z] = pick([vbuf[b] for b in range(ny)], gid_y)
    for d in range(1, nz):
        z_copy(zv, zvs, zvr, d).start()
    pull_bands(2, 5)

    l_wait()
    logits = total_of(lbuf, nt)
    place = lax.broadcasted_iota(jnp.int32, (8, HEAD), 0) * HEAD + lax.broadcasted_iota(jnp.int32, (8, HEAD), 1)
    valid = place < CLASSES
    logits = jnp.where(valid, logits, -jnp.inf)

    def all_sum(x):
        return jnp.sum(jnp.sum(x, 0, keepdims=True), 1, keepdims=True)

    top = jnp.max(jnp.max(logits, 0, keepdims=True), 1, keepdims=True)
    probs = jnp.exp(logits - top)
    probs = probs / all_sum(probs)
    pbuf[f] = probs
    p_start()

    pull_bands(5, ny)
    for d in range(1, nz):
        z_copy(zv, zvs, zvr, d).wait_recv()
    for c in v_ends():
        c.wait_recv()
    vg = pick([zv[i] for i in range(nz)], gid_z)
    e_bf[...] = e_acc[...].astype(BF16)
    ones_rows = jnp.ones((16, rows), BF16)
    for h in range(hc):
        cols = slice(h * HEAD, (h + 1) * HEAD)
        eg = eg_acc[h].astype(BF16)
        v = v_head(h)
        m = dot(v, e_bf[h, ROW : ROW + rows, :], TN) + dot(vg[:, cols], eg, TN)
        m = m + dot(vend[:ROW, cols], e_bf[h, :ROW, :], TN)
        m = m + dot(vend[ROW:, cols], e_bf[h, ROW + rows :, :], TN)
        middle = dot(v, ones_rows, (((0,), (1,)), ((), ())))[:, :1] * (1.0 / rows)
        total = jnp.sum(e_bf[h].astype(F32), 0, keepdims=True) + jnp.sum(eg.astype(F32), 0, keepdims=True)
        m = m - middle * total
        high = m.astype(BF16)
        pull[h, :, :HEAD] = high
        pull[h, :, HEAD:] = (m - high.astype(F32)).astype(BF16)

    p_wait()
    mean = total_of(pbuf, nf) * (1.0 / nf)
    log_mean = jnp.where(valid, jnp.log(mean), 0.0)
    entropy = -all_sum(jnp.where(valid, mean * log_mean, 0.0))
    ent_ref[...] = entropy
    upstream = jnp.where(valid, -(log_mean + 1.0) * (1.0 / nf), 0.0)
    dlogits = probs * (upstream - all_sum(probs * upstream))
    dlogits = jnp.concatenate([dlogits[i : i + 1] for i in range(8)], 1)
    dpooled = row_dot(dlogits, rpad[...], NT) * (1.0 / tokens)
    wbuf[f] = jnp.zeros((8, HEAD), F32)
    for h in range(hc):
        cols = slice(h * HEAD, (h + 1) * HEAD)
        got = row_dot(dpooled[:, cols], pull[h], NN)
        wbuf[f, h : h + 1, :] = (got[:, :HEAD] + got[:, HEAD:]) * SCALE
    w_start()
    w_wait()
    tbuf[t] = total_of(wbuf, nf)
    t_start()
    t_wait()
    for i in range(ny):
        got = None
        for j in range(nz):
            row = jnp.where(chip % 2 == 0, j, nz - 1 - j)
            part = tbuf[row * ny + i]
            got = part if got is None else got + part
        w_out[i * hc : (i + 1) * hc, :] = got[:hc]

    for d in far_first:
        v_copy(d).wait_send()
    for d in range(1, nz):
        z_copy(zk, zks, zkr, d).wait_send()
        z_copy(zv, zvs, zvr, d).wait_send()
        z_copy(zw, zws, zwr, d).wait_send()
    for c in k_ends() + v_ends():
        c.wait_send()

    @pl.when(holder)
    def _():
        mirror_copy().wait_send()
        for d in lines:
            x_copy(r_ref, d).wait_send()

    @pl.when(relay)
    def _():
        for d in lines:
            x_copy(rraw.at[mine], d).wait_send()

    twin_copy(mine).wait_send()
    l_sent()
    p_sent()
    w_sent()
    t_sent()


def make_body(ny):
    def body(queries, keys, values, readout, global_block, q_gain, k_gain):
        nf, nt = lax.axis_size("fsdp"), lax.axis_size("tok")
        nz = nt // ny
        heads = q_gain.shape[0] // HEAD
        hc = heads // ny
        width = hc * HEAD
        rows = ny * BAND
        padded = rows + 2 * ROW
        tokens = nt * BAND
        dma = pltpu.SemaphoreType.DMA
        vmem = pltpu.VMEM
        scratch = [
            pltpu.SMEM((1,), jnp.int32),
            vmem((heads, HEAD), F32),
            vmem((heads, HEAD), F32),
            vmem((padded, width), BF16),
            vmem((ny, BAND, width), BF16),
            vmem((2 * ROW, width), BF16),
            vmem((ny, BAND, width), BF16),
            vmem((hc, padded, 2 * HEAD), BF16),
            vmem((hc, BAND, 2 * HEAD), BF16),
            vmem((nz, BAND, width), BF16),
            vmem((nz, BAND, width), BF16),
            vmem((nz, 8, HEAD), F32),
            vmem((width, CLASSES), BF16),
            vmem((width, PAD), BF16),
            vmem((ny, hc, BAND, SEEN), BF16),
            vmem((ny, hc, BAND, HEAD), BF16),
            vmem((ny, hc, 8, SEEN), F32),
            vmem((hc, padded, HEAD), F32),
            vmem((hc, BAND, HEAD), F32),
            vmem((hc, padded, HEAD), BF16),
            vmem((hc, HEAD, 2 * HEAD), BF16),
            vmem((nt, 8, HEAD), F32),
            vmem((nf, 8, HEAD), F32),
            vmem((nf, 8, HEAD), F32),
            vmem((nt, 8, HEAD), F32),
        ]
        scratch += [dma((ny,))] * 6 + [dma((7,))] + [dma((nz,))] * 4 + [dma((2,))] * 4 + [dma((nz,))] * 2
        scratch += [dma((nf // 4,)), dma((1,)), dma, dma]
        scratch += [dma((nt,))] * 2 + [dma((nf,))] * 4 + [dma((nt,))] * 2
        hbm = pl.BlockSpec(memory_space=pl.ANY)
        whole = pl.BlockSpec(memory_space=pltpu.VMEM)
        entropy, total = pl.pallas_call(
            functools.partial(kernel, ny, nz, nf, hc, tokens),
            out_shape=(
                jax.ShapeDtypeStruct((1, 1), F32),
                jax.ShapeDtypeStruct((heads, HEAD), F32),
            ),
            in_specs=[hbm] * 7,
            out_specs=(whole, whole),
            scratch_shapes=scratch,
            compiler_params=pltpu.CompilerParams(
                collective_id=0, has_side_effects=True, vmem_limit_bytes=60 * 2**20
            ),
            name="adapt",
        )(
            global_block,
            queries,
            keys,
            values,
            readout,
            q_gain.reshape(heads, HEAD),
            k_gain.reshape(heads, HEAD),
        )
        total = total.reshape(-1)
        return entropy.reshape(()), total / q_gain, total / k_gain

    return body


def solution(mesh):
    in_specs = (
        P("fsdp", "tok", None),
        P("fsdp", "tok", None),
        P("fsdp", "tok", None),
        P("fsdp", None),
        P("fsdp"),
        P(),
        P(),
    )
    out_specs = (P(), P(), P())
    return jax.shard_map(make_body(Y), mesh=mesh, in_specs=in_specs, out_specs=out_specs, check_vma=False)
```

```python
import functools

import jax
import jax.numpy as jnp
from jax import lax
from jax.experimental import pallas as pl
from jax.experimental.pallas import tpu as pltpu
from jax.sharding import PartitionSpec as P

HEAD = 128
ROW = 64
BAND = 128
CLASSES = 1000
PAD = 1024
WIN = BAND + 2 * ROW
SEEN = WIN + BAND
Y = 8
MESH = pl.DeviceIdType.MESH
F32 = jnp.float32
BF16 = jnp.bfloat16
NT = (((1,), (1,)), ((), ()))
NN = (((1,), (0,)), ((), ()))
TN = (((0,), (0,)), ((), ()))
SCALE = HEAD**-0.5


def dot(a, b, dims):
    return lax.dot_general(a, b, dims, preferred_element_type=F32)


def normalize(x, gain):
    x = x.astype(F32)
    x = x - jnp.mean(x, -1, keepdims=True)
    var = jnp.mean(x * x, -1, keepdims=True)
    return (x * lax.rsqrt(var + 1e-06) * gain).astype(BF16)


def split3(x):
    x = jnp.broadcast_to(x, (16, x.shape[1]))
    high = x.astype(BF16).astype(F32)
    rest = x - high
    mid = rest.astype(BF16).astype(F32)
    low = rest - mid
    row = lax.broadcasted_iota(jnp.int32, x.shape, 0)
    out = jnp.where(row == 0, high, jnp.where(row == 1, mid, jnp.where(row == 2, low, 0.0)))
    return out.astype(BF16)


def row_dot(x, b, dims):
    return jnp.sum(dot(split3(x), b, dims), 0, keepdims=True)


def kernel(
    ny, nz, nf, hc, tokens,
    gid_hbm, q_ref, k_ref, v_ref, r_ref, qg_hbm, kg_hbm,
    ent_ref, w_out,
    gid_ref, qg_ref, kg_ref,
    kpad, vbuf, vend, qbuf, knpad, kng, zk, zv, zw, rraw, rpad, att, qn_s, w_s, e_acc, eg_acc, e_bf, pull,
    lbuf, pbuf, wbuf, tbuf,
    ks, kr, vs, vr, qs, qr, local, zks, zkr, zvs, zvr, hks, hkr, hvs, hvr, zws, zwr,
    rs, rr, fs, fr, lsem, lrem, psem, prem, wsem, wrem, tsem, trem,
):
    nt = nz * ny
    f, t = lax.axis_index("fsdp"), lax.axis_index("tok")
    z, y = t // ny, t % ny
    core = f % 2
    width = hc * HEAD
    rows = ny * BAND
    shard = r_ref.shape[0]

    def copy(src, dst, ssem, rsem, dev):
        return pltpu.make_async_remote_copy(
            src_ref=src, dst_ref=dst, send_sem=ssem, recv_sem=rsem, device_id=dev, device_id_type=MESH
        )

    def chunk(c):
        return pl.ds(pl.multiple_of(c * width, HEAD), width)

    def band_rows(b):
        return pl.ds(pl.multiple_of(ROW + b * BAND, ROW), BAND)

    own_k = pltpu.make_async_copy(k_ref.at[0, :, chunk(y)], kpad.at[band_rows(y)], local.at[0])
    own_v = pltpu.make_async_copy(v_ref.at[0, :, chunk(y)], vbuf.at[y], local.at[1])
    own_q = pltpu.make_async_copy(q_ref.at[0, :, chunk(y)], qbuf.at[y], local.at[2])
    own_k.start()
    own_v.start()
    own_q.start()

    small = [
        pltpu.make_async_copy(gid_hbm, gid_ref, local.at[4]),
        pltpu.make_async_copy(qg_hbm, qg_ref, local.at[5]),
        pltpu.make_async_copy(kg_hbm, kg_ref, local.at[6]),
    ]
    for c in small:
        c.start()

    chip = f // 2
    mirror_t = (nz - 1 - z) * ny + y

    def wrap(i, n):
        return jnp.where(i >= n, i - n, i)

    def f_dev(p):
        return (p, jnp.where((p // 2) % 2 == chip % 2, t, mirror_t))

    def t_peers(act):
        def column(k, carry):
            d = jnp.where(k % 2 == 1, ny // 2 - (k + 1) // 2, ny // 2 + k // 2)
            far_y = wrap(y + d, ny)
            for i in range(nz):
                p = wrap(z + i, nz) * ny + far_y
                act(p, (f, p), i * ny + d)
            return carry

        lax.fori_loop(0, ny - 1, column, 0)
        for i in range(1, nz):
            p = wrap(z + i, nz) * ny + y
            act(p, (f, p), i * ny)

    def f_peers(act):
        nx = nf // 4
        x = f // 4
        steps = sorted(range(nf), key=lambda s: -(2 * min(s // 4, nx - s // 4) + 3 * (s // 2 % 2)))
        for s in steps:
            if s:
                other = chip % 2
                if s // 2 % 2:
                    other = 1 - other
                twin = 1 - core if s % 2 else core
                p = (wrap(x + s // 4, nx) * 2 + other) * 2 + twin
                act(p, f_dev(p), s)

    barrier = pltpu.get_barrier_semaphore()

    def greet(dev):
        pl.semaphore_signal(barrier, inc=1, device_id=dev, device_id_type=MESH)

    t_peers(lambda slot, dev, number: greet(dev))
    f_peers(lambda slot, dev, number: greet(dev))
    pl.semaphore_wait(barrier, nt - 1 + nf - 1)

    order = [0]
    for d in range(1, ny // 2 + 1):
        order.append(d)
        if ny - d != d:
            order.append(ny - d)

    def y_dev(d):
        return (f, z * ny + (y + d) % ny)

    def k_copy(d):
        p = (y + d) % ny
        return copy(k_ref.at[0, :, chunk(p)], kpad.at[band_rows(y)], ks.at[d], kr.at[d], y_dev(d))

    def v_copy(d):
        p = (y + d) % ny
        return copy(v_ref.at[0, :, chunk(p)], vbuf.at[y], vs.at[d], vr.at[d], y_dev(d))

    def q_copy(d):
        p = (y + d) % ny
        return copy(q_ref.at[0, :, chunk(p)], qbuf.at[y], qs.at[d], qr.at[d], y_dev(d))

    far_first = order[:0:-1]
    for d in far_first:
        k_copy(d).start()

    mine = pl.ds(pl.multiple_of(core * shard, 64), shard)
    holder = chip == y
    relay = (chip // 2 == y // 2) & (chip != y)
    leaf = chip // 2 != y // 2
    lines = range(1, nf // 4)

    def x_copy(src, d):
        return copy(src, rraw.at[mine], rs.at[d], rr.at[0], ((f + 4 * d) % nf, t))

    def mirror_copy():
        return copy(r_ref, rraw.at[mine], rs.at[0], rr.at[0], f_dev(f + 2 - 4 * (chip % 2)))

    def r_local():
        return pltpu.make_async_copy(r_ref, rraw.at[mine], local.at[3])

    @pl.when(holder)
    def _():
        mirror_copy().start()
        for d in lines:
            x_copy(r_ref, d).start()
        r_local().start()

    for d in far_first:
        k_copy(d).wait_send()
    for d in far_first:
        q_copy(d).start()

    own_k.wait()
    for d in far_first:
        k_copy(d).wait_recv()
    for c in small:
        c.wait()
    gid = gid_ref[0]
    gid_y, gid_z = lax.rem(gid, ny), lax.div(gid, ny)

    def pick(parts, want):
        out = None
        for i, part in enumerate(parts):
            part = part.astype(F32) * jnp.where(want == i, 1.0, 0.0)
            out = part if out is None else out + part
        return out.astype(BF16)

    def z_dev(d):
        return (f, ((z + d) % nz) * ny + y)

    def z_copy(buf, ssem, rsem, d):
        return copy(buf.at[z], buf.at[z], ssem.at[d], rsem.at[d], z_dev(d))

    def k_ends():
        up = copy(kpad.at[pl.ds(rows, ROW)], kpad.at[pl.ds(0, ROW)], hks.at[0], hkr.at[0], z_dev(1))
        down = copy(kpad.at[pl.ds(ROW, ROW)], kpad.at[pl.ds(ROW + rows, ROW)], hks.at[1], hkr.at[1], z_dev(nz - 1))
        return up, down

    def v_ends():
        low, high = pl.ds(0, ROW), pl.ds(ROW, ROW)
        up = copy(vbuf.at[ny - 1, high], vend.at[low], hvs.at[0], hvr.at[0], z_dev(1))
        down = copy(vbuf.at[0, low], vend.at[high], hvs.at[1], hvr.at[1], z_dev(nz - 1))
        return up, down

    zk[z] = pick([kpad[ROW + b * BAND : ROW + (b + 1) * BAND, :] for b in range(ny)], gid_y)
    for d in range(1, nz):
        z_copy(zk, zks, zkr, d).start()
    for c in k_ends():
        c.start()

    q_gain = [qg_ref[pl.ds(y * hc + h, 1), :] for h in range(hc)]
    k_gain = [kg_ref[pl.ds(y * hc + h, 1), :] for h in range(hc)]
    knpad[:, :, HEAD:] = jnp.ones((hc, rows + 2 * ROW, HEAD), BF16)
    kng[:, :, HEAD:] = jnp.ones((hc, BAND, HEAD), BF16)

    def norm_rows(at, size):
        for h in range(hc):
            knpad[h, at, :HEAD] = normalize(kpad[at, h * HEAD : (h + 1) * HEAD], k_gain[h])

    def norm_band(b, carry):
        norm_rows(band_rows(b), BAND)
        return carry

    lax.fori_loop(0, ny, norm_band, 0)

    for d in far_first:
        q_copy(d).wait_send()
    for d in far_first:
        v_copy(d).start()

    for d in range(1, nz):
        z_copy(zk, zks, zkr, d).wait_recv()
    for c in k_ends():
        c.wait_recv()
    norm_rows(pl.ds(0, ROW), ROW)
    norm_rows(pl.ds(ROW + rows, ROW), ROW)
    kg_raw = pick([zk[i] for i in range(nz)], gid_z)
    for h in range(hc):
        kng[h, :, :HEAD] = normalize(kg_raw[:, h * HEAD : (h + 1) * HEAD], k_gain[h])

    @pl.when(relay)
    def _():
        mirror_copy().wait_recv()
        for d in lines:
            x_copy(rraw.at[mine], d).start()

    ones16 = jnp.ones((16, BAND), BF16)
    lane = lax.broadcasted_iota(jnp.int32, (BAND, WIN), 1)

    def band(b):
        low = jnp.where((z == 0) & (b == 0), ROW, 0)
        high = jnp.where((z == nz - 1) & (b == ny - 1), ROW + BAND, WIN)
        usable = (lane >= low) & (lane < high)
        window = pl.ds(pl.multiple_of(b * BAND, BAND), WIN)
        for h in range(hc):
            qn = normalize(qbuf[b, :, h * HEAD : (h + 1) * HEAD], q_gain[h])
            qn_s[b, h] = qn
            near = dot(qn, knpad[h, window, :HEAD], NT) * SCALE
            far = dot(qn, kng[h, :, :HEAD], NT) * SCALE
            near = jnp.where(usable, near, -1e30)
            top = jnp.maximum(jnp.max(near, -1, keepdims=True), jnp.max(far, -1, keepdims=True))
            near = jnp.exp(near - top)
            far = jnp.exp(far - top)
            total = jnp.sum(near, -1, keepdims=True) + jnp.sum(far, -1, keepdims=True)
            inv = 1.0 / total
            near = (near * inv).astype(BF16)
            far = (far * inv).astype(BF16)
            att[b, h, :, :WIN] = near
            att[b, h, :, WIN:] = far
            w_s[b, h, :, :WIN] = dot(ones16, near, NN)[:8]
            w_s[b, h, :, WIN:] = dot(ones16, far, NN)[:8]

    own_q.wait()
    for d in order:
        if d:
            q_copy(ny - d).wait_recv()
        band((y + d) % ny)

    half = lax.broadcasted_iota(jnp.int32, (1, HEAD), 1) < ROW
    given = []
    zw[z] = jnp.zeros((8, HEAD), F32)
    for h in range(hc):
        parts = [jnp.zeros((1, HEAD), F32) for _ in range(ny + 1)]
        far = jnp.zeros((1, HEAD), F32)
        for b in range(ny):
            parts[b] = parts[b] + w_s[b, h, 0:1, :HEAD]
            parts[b + 1] = parts[b + 1] + w_s[b, h, 0:1, HEAD:WIN]
            far = far + w_s[b, h, 0:1, WIN:]
        given.append(parts)
        zw[z, h : h + 1, :] = far
        zw[z, hc + h : hc + h + 1, :] = jnp.where(half, parts[0], parts[ny])
    for d in range(1, nz):
        z_copy(zw, zws, zwr, d).start()

    @pl.when(holder)
    def _():
        r_local().wait()

    if nf > 4:

        @pl.when(leaf)
        def _():
            mirror_copy().wait_recv()

    def twin_copy(at):
        return copy(rraw.at[at], rraw.at[at], fs, fr, (f + 1 - 2 * core, t))

    twin_copy(mine).start()

    e_acc[...] = jnp.zeros_like(e_acc)
    eg_acc[...] = jnp.zeros_like(eg_acc)

    def pulled(b, carry):
        window = pl.ds(pl.multiple_of(b * BAND, BAND), WIN)
        for h in range(hc):
            near = att[b, h, :, :WIN]
            far = att[b, h, :, WIN:]
            kn = knpad[h, window, :]
            kg = kng[h]
            mean_key = dot(near, kn, NN) + dot(far, kg, NN)
            qn = qn_s[b, h]
            qk = qn.astype(F32) * (mean_key[:, :HEAD] / mean_key[:, HEAD:])
            qk_high = qk.astype(BF16)
            qk_low = (qk - qk_high.astype(F32)).astype(BF16)
            right = jnp.concatenate([qn, qk_high, qk_low], 1)
            got = dot(near, right, TN)
            e_acc[h, window, :] += (
                kn[:, :HEAD].astype(F32) * got[:, :HEAD] - got[:, HEAD : 2 * HEAD] - got[:, 2 * HEAD :]
            )
            got = dot(far, right, TN)
            eg_acc[h] += kg[:, :HEAD].astype(F32) * got[:, :HEAD] - got[:, HEAD : 2 * HEAD] - got[:, 2 * HEAD :]
        return carry

    def pull_bands(first, last):
        lax.fori_loop(min(first, ny), min(last, ny), pulled, 0)

    pull_bands(0, 4)

    other = pl.ds(pl.multiple_of((1 - core) * shard, 64), shard)
    twin_copy(other).wait_recv()
    rpad[:, CLASSES // HEAD * HEAD :] = jnp.zeros((width, PAD - CLASSES // HEAD * HEAD), BF16)
    rpad[:, :CLASSES] = rraw[...]

    for d in range(1, nz):
        z_copy(zw, zws, zwr, d).wait_recv()
    below = zw[lax.rem(z + nz - 1, nz)]
    above = zw[lax.rem(z + 1, nz)]
    all_far = zw[0]
    for i in range(1, nz):
        all_far = all_far + zw[i]
    weights = []
    for h in range(hc):
        parts = given[h]
        parts[0] = parts[0] + below[hc + h : hc + h + 1]
        parts[ny] = parts[ny] + above[hc + h : hc + h + 1]
        own = []
        for b in range(ny):
            tile = jnp.concatenate([parts[b][:, ROW:], parts[b + 1][:, :ROW]], 1)
            own.append(tile + all_far[h : h + 1] * jnp.where(gid == z * ny + b, 1.0, 0.0))
        weights.append(split3(jnp.concatenate(own, 1)))

    def v_head(h):
        return vbuf[:, :, h * HEAD : (h + 1) * HEAD].reshape(rows, HEAD)

    own_v.wait()
    for d in far_first:
        v_copy(d).wait_recv()
    pooled = [jnp.sum(dot(weights[h], v_head(h), NN), 0, keepdims=True) for h in range(hc)]
    pooled = jnp.concatenate(pooled, 1) * (1.0 / tokens)
    logits = row_dot(pooled, rpad[...], NN)
    for i in range(8):
        lbuf[t, i : i + 1, :] = logits[:, i * HEAD : (i + 1) * HEAD]

    def exchange(buf, me, peers, ssem, rsem):
        def out(dev, number):
            return copy(buf.at[me], buf.at[me], ssem.at[number], rsem.at[me], dev)

        def come(slot, dev):
            return copy(buf.at[slot], buf.at[slot], ssem.at[0], rsem.at[slot], dev)

        def start():
            peers(lambda slot, dev, number: out(dev, number).start())

        def wait():
            peers(lambda slot, dev, number: come(slot, dev).wait_recv())

        def wait_sent():
            peers(lambda slot, dev, number: out(dev, number).wait_send())

        return start, wait, wait_sent

    def total_of(buf, n):
        out = buf[0]
        for i in range(1, n):
            out = out + buf[i]
        return out

    l_start, l_wait, l_sent = exchange(lbuf, t, t_peers, lsem, lrem)
    p_start, p_wait, p_sent = exchange(pbuf, f, f_peers, psem, prem)
    w_start, w_wait, w_sent = exchange(wbuf, f, f_peers, wsem, wrem)
    t_start, t_wait, t_sent = exchange(tbuf, t, t_peers, tsem, trem)
    l_start()

    for c in v_ends():
        c.start()
    zv[z] = pick([vbuf[b] for b in range(ny)], gid_y)
    for d in range(1, nz):
        z_copy(zv, zvs, zvr, d).start()
    pull_bands(4, 7)

    l_wait()
    logits = total_of(lbuf, nt)
    place = lax.broadcasted_iota(jnp.int32, (8, HEAD), 0) * HEAD + lax.broadcasted_iota(jnp.int32, (8, HEAD), 1)
    valid = place < CLASSES
    logits = jnp.where(valid, logits, -jnp.inf)

    def all_sum(x):
        return jnp.sum(jnp.sum(x, 0, keepdims=True), 1, keepdims=True)

    top = jnp.max(jnp.max(logits, 0, keepdims=True), 1, keepdims=True)
    probs = jnp.exp(logits - top)
    probs = probs / all_sum(probs)
    pbuf[f] = probs
    p_start()

    pull_bands(7, ny)
    for d in range(1, nz):
        z_copy(zv, zvs, zvr, d).wait_recv()
    for c in v_ends():
        c.wait_recv()
    vg = pick([zv[i] for i in range(nz)], gid_z)
    e_bf[...] = e_acc[...].astype(BF16)
    ones_rows = jnp.ones((16, rows), BF16)
    for h in range(hc):
        cols = slice(h * HEAD, (h + 1) * HEAD)
        eg = eg_acc[h].astype(BF16)
        v = v_head(h)
        m = dot(v, e_bf[h, ROW : ROW + rows, :], TN) + dot(vg[:, cols], eg, TN)
        m = m + dot(vend[:ROW, cols], e_bf[h, :ROW, :], TN)
        m = m + dot(vend[ROW:, cols], e_bf[h, ROW + rows :, :], TN)
        middle = dot(v, ones_rows, (((0,), (1,)), ((), ())))[:, :1] * (1.0 / rows)
        total = jnp.sum(e_bf[h].astype(F32), 0, keepdims=True) + jnp.sum(eg.astype(F32), 0, keepdims=True)
        m = m - middle * total
        high = m.astype(BF16)
        pull[h, :, :HEAD] = high
        pull[h, :, HEAD:] = (m - high.astype(F32)).astype(BF16)

    p_wait()
    mean = total_of(pbuf, nf) * (1.0 / nf)
    log_mean = jnp.where(valid, jnp.log(mean), 0.0)
    entropy = -all_sum(jnp.where(valid, mean * log_mean, 0.0))
    ent_ref[...] = jnp.broadcast_to(entropy, ent_ref.shape)
    upstream = jnp.where(valid, -(log_mean + 1.0) * (1.0 / nf), 0.0)
    dlogits = probs * (upstream - all_sum(probs * upstream))
    dlogits = jnp.concatenate([dlogits[i : i + 1] for i in range(8)], 1)
    dpooled = row_dot(dlogits, rpad[...], NT) * (1.0 / tokens)
    wbuf[f] = jnp.zeros((8, HEAD), F32)
    for h in range(hc):
        cols = slice(h * HEAD, (h + 1) * HEAD)
        got = row_dot(dpooled[:, cols], pull[h], NN)
        wbuf[f, h : h + 1, :] = (got[:, :HEAD] + got[:, HEAD:]) * SCALE
    w_start()
    w_wait()
    tbuf[t] = total_of(wbuf, nf)
    t_start()
    t_wait()
    for i in range(ny):
        got = None
        for j in range(nz):
            row = jnp.where(chip % 2 == 0, j, nz - 1 - j)
            part = tbuf[row * ny + i]
            got = part if got is None else got + part
        w_out[i * hc : (i + 1) * hc, :] = got[:hc]

    for d in far_first:
        v_copy(d).wait_send()
    for d in range(1, nz):
        z_copy(zk, zks, zkr, d).wait_send()
        z_copy(zv, zvs, zvr, d).wait_send()
        z_copy(zw, zws, zwr, d).wait_send()
    for c in k_ends() + v_ends():
        c.wait_send()

    @pl.when(holder)
    def _():
        mirror_copy().wait_send()
        for d in lines:
            x_copy(r_ref, d).wait_send()

    @pl.when(relay)
    def _():
        for d in lines:
            x_copy(rraw.at[mine], d).wait_send()

    twin_copy(mine).wait_send()
    l_sent()
    p_sent()
    w_sent()
    t_sent()


def make_body(ny):
    def body(queries, keys, values, readout, global_block, q_gain, k_gain):
        nf, nt = lax.axis_size("fsdp"), lax.axis_size("tok")
        nz = nt // ny
        heads = q_gain.shape[0] // HEAD
        hc = heads // ny
        width = hc * HEAD
        rows = ny * BAND
        padded = rows + 2 * ROW
        tokens = nt * BAND
        dma = pltpu.SemaphoreType.DMA
        vmem = pltpu.VMEM
        scratch = [
            pltpu.SMEM((1,), jnp.int32),
            vmem((heads, HEAD), F32),
            vmem((heads, HEAD), F32),
            vmem((padded, width), BF16),
            vmem((ny, BAND, width), BF16),
            vmem((2 * ROW, width), BF16),
            vmem((ny, BAND, width), BF16),
            vmem((hc, padded, 2 * HEAD), BF16),
            vmem((hc, BAND, 2 * HEAD), BF16),
            vmem((nz, BAND, width), BF16),
            vmem((nz, BAND, width), BF16),
            vmem((nz, 8, HEAD), F32),
            vmem((width, CLASSES), BF16),
            vmem((width, PAD), BF16),
            vmem((ny, hc, BAND, SEEN), BF16),
            vmem((ny, hc, BAND, HEAD), BF16),
            vmem((ny, hc, 8, SEEN), F32),
            vmem((hc, padded, HEAD), F32),
            vmem((hc, BAND, HEAD), F32),
            vmem((hc, padded, HEAD), BF16),
            vmem((hc, HEAD, 2 * HEAD), BF16),
            vmem((nt, 8, HEAD), F32),
            vmem((nf, 8, HEAD), F32),
            vmem((nf, 8, HEAD), F32),
            vmem((nt, 8, HEAD), F32),
        ]
        scratch += [dma((ny,))] * 6 + [dma((7,))] + [dma((nz,))] * 4 + [dma((2,))] * 4 + [dma((nz,))] * 2
        scratch += [dma((nf // 4,)), dma((1,)), dma, dma]
        scratch += [dma((nt,))] * 2 + [dma((nf,))] * 4 + [dma((nt,))] * 2
        hbm = pl.BlockSpec(memory_space=pl.ANY)
        in_hbm = pl.BlockSpec(memory_space=pltpu.HBM)
        whole = pl.BlockSpec(memory_space=pltpu.VMEM)
        entropy, total = pl.pallas_call(
            functools.partial(kernel, ny, nz, nf, hc, tokens),
            out_shape=(
                jax.ShapeDtypeStruct((8, HEAD), F32),
                jax.ShapeDtypeStruct((heads, HEAD), F32),
            ),
            in_specs=[in_hbm, hbm, hbm, hbm, hbm, in_hbm, in_hbm],
            out_specs=(whole, whole),
            scratch_shapes=scratch,
            compiler_params=pltpu.CompilerParams(
                collective_id=0, has_side_effects=True, vmem_limit_bytes=60 * 2**20
            ),
            name="adapt",
        )(
            global_block,
            queries,
            keys,
            values,
            readout,
            q_gain.reshape(heads, HEAD),
            k_gain.reshape(heads, HEAD),
        )
        total = total.reshape(-1)
        return entropy[0, 0], total / q_gain, total / k_gain

    return body


def solution(mesh):
    in_specs = (
        P("fsdp", "tok", None),
        P("fsdp", "tok", None),
        P("fsdp", "tok", None),
        P("fsdp", None),
        P("fsdp"),
        P(),
        P(),
    )
    out_specs = (P(), P(), P())
    return jax.shard_map(make_body(Y), mesh=mesh, in_specs=in_specs, out_specs=out_specs, check_vma=False)
```

```python
import functools

import jax
import jax.numpy as jnp
from jax import lax
from jax.experimental import pallas as pl
from jax.experimental.pallas import tpu as pltpu
from jax.sharding import PartitionSpec as P

HEAD = 128
ROW = 64
BAND = 128
CLASSES = 1000
PAD = 1024
WIN = BAND + 2 * ROW
SEEN = WIN + BAND
Y = 8
MESH = pl.DeviceIdType.MESH
F32 = jnp.float32
BF16 = jnp.bfloat16
NT = (((1,), (1,)), ((), ()))
NN = (((1,), (0,)), ((), ()))
TN = (((0,), (0,)), ((), ()))
SCALE = HEAD**-0.5


def dot(a, b, dims):
    return lax.dot_general(a, b, dims, preferred_element_type=F32)


def normalize(x, gain):
    x = x.astype(F32)
    x = x - jnp.mean(x, -1, keepdims=True)
    var = jnp.mean(x * x, -1, keepdims=True)
    return (x * lax.rsqrt(var + 1e-06) * gain).astype(BF16)


def split3(x):
    x = jnp.broadcast_to(x, (16, x.shape[1]))
    high = x.astype(BF16).astype(F32)
    rest = x - high
    mid = rest.astype(BF16).astype(F32)
    low = rest - mid
    row = lax.broadcasted_iota(jnp.int32, x.shape, 0)
    out = jnp.where(row == 0, high, jnp.where(row == 1, mid, jnp.where(row == 2, low, 0.0)))
    return out.astype(BF16)


def row_dot(x, b, dims):
    return jnp.sum(dot(split3(x), b, dims), 0, keepdims=True)


def kernel(
    ny, nz, nf, hc, tokens,
    gid_hbm, q_ref, k_ref, v_ref, r_ref, qg_hbm, kg_hbm,
    ent_ref, w_out,
    gid_ref, qg_ref, kg_ref,
    kpad, vbuf, vend, qbuf, knpad, kng, zk, zv, zw, rraw, rpad, att, qn_s, w_s, e_acc, eg_acc, e_bf, pull,
    lbuf, pbuf, wbuf, tbuf,
    ks, kr, vs, vr, qs, qr, local, zks, zkr, zvs, zvr, hks, hkr, hvs, hvr, zws, zwr,
    rs, rr, fs, fr, lsem, lrem, psem, prem, wsem, wrem, tsem, trem,
):
    nt = nz * ny
    f, t = lax.axis_index("fsdp"), lax.axis_index("tok")
    z, y = t // ny, t % ny
    core = f % 2
    width = hc * HEAD
    rows = ny * BAND
    shard = r_ref.shape[0]

    def copy(src, dst, ssem, rsem, dev):
        return pltpu.make_async_remote_copy(
            src_ref=src, dst_ref=dst, send_sem=ssem, recv_sem=rsem, device_id=dev, device_id_type=MESH
        )

    def chunk(c):
        return pl.ds(pl.multiple_of(c * width, HEAD), width)

    def band_rows(b):
        return pl.ds(pl.multiple_of(ROW + b * BAND, ROW), BAND)

    own_k = pltpu.make_async_copy(k_ref.at[0, :, chunk(y)], kpad.at[band_rows(y)], local.at[0])
    own_v = pltpu.make_async_copy(v_ref.at[0, :, chunk(y)], vbuf.at[y], local.at[1])
    own_q = pltpu.make_async_copy(q_ref.at[0, :, chunk(y)], qbuf.at[y], local.at[2])
    own_k.start()
    own_v.start()
    own_q.start()

    small = [
        pltpu.make_async_copy(gid_hbm, gid_ref, local.at[4]),
        pltpu.make_async_copy(qg_hbm, qg_ref, local.at[5]),
        pltpu.make_async_copy(kg_hbm, kg_ref, local.at[6]),
    ]
    for c in small:
        c.start()

    chip = f // 2
    mirror_t = (nz - 1 - z) * ny + y

    def wrap(i, n):
        return jnp.where(i >= n, i - n, i)

    def f_dev(p):
        return (p, jnp.where((p // 2) % 2 == chip % 2, t, mirror_t))

    def t_peers(act, far_last=False):
        def column(k, carry):
            if far_last:
                k = ny - 2 - k
            d = jnp.where(k % 2 == 1, ny // 2 - (k + 1) // 2, ny // 2 + k // 2)
            far_y = wrap(y + d, ny)
            for i in range(nz):
                p = wrap(z + i, nz) * ny + far_y
                act(p, (f, p), i * ny + d)
            return carry

        def own_column():
            for i in range(1, nz):
                p = wrap(z + i, nz) * ny + y
                act(p, (f, p), i * ny)

        if far_last:
            own_column()
        lax.fori_loop(0, ny - 1, column, 0)
        if not far_last:
            own_column()

    def f_peers(act, far_last=False):
        nx = nf // 4
        x = f // 4
        steps = sorted(range(1, nf), key=lambda s: -(2 * min(s // 4, nx - s // 4) + 3 * (s // 2 % 2)))
        for s in steps[::-1] if far_last else steps:
            other = chip % 2
            if s // 2 % 2:
                other = 1 - other
            twin = 1 - core if s % 2 else core
            p = (wrap(x + s // 4, nx) * 2 + other) * 2 + twin
            act(p, f_dev(p), s)

    barrier = pltpu.get_barrier_semaphore()

    def greet(dev):
        pl.semaphore_signal(barrier, inc=1, device_id=dev, device_id_type=MESH)

    t_peers(lambda slot, dev, number: greet(dev))
    f_peers(lambda slot, dev, number: greet(dev))
    pl.semaphore_wait(barrier, nt - 1 + nf - 1)

    order = [0]
    for d in range(1, ny // 2 + 1):
        order.append(d)
        if ny - d != d:
            order.append(ny - d)

    def y_dev(d):
        return (f, z * ny + (y + d) % ny)

    def k_copy(d):
        p = (y + d) % ny
        return copy(k_ref.at[0, :, chunk(p)], kpad.at[band_rows(y)], ks.at[d], kr.at[d], y_dev(d))

    def v_copy(d):
        p = (y + d) % ny
        return copy(v_ref.at[0, :, chunk(p)], vbuf.at[y], vs.at[d], vr.at[d], y_dev(d))

    def q_copy(d):
        p = (y + d) % ny
        return copy(q_ref.at[0, :, chunk(p)], qbuf.at[y], qs.at[d], qr.at[d], y_dev(d))

    far_first = order[:0:-1]
    for d in far_first:
        k_copy(d).start()

    mine = pl.ds(pl.multiple_of(core * shard, 64), shard)
    holder = chip == y
    relay = (chip // 2 == y // 2) & (chip != y)
    leaf = chip // 2 != y // 2
    lines = range(1, nf // 4)

    def x_copy(src, d):
        return copy(src, rraw.at[mine], rs.at[d], rr.at[0], ((f + 4 * d) % nf, t))

    def mirror_copy():
        return copy(r_ref, rraw.at[mine], rs.at[0], rr.at[0], f_dev(f + 2 - 4 * (chip % 2)))

    def r_local():
        return pltpu.make_async_copy(r_ref, rraw.at[mine], local.at[3])

    @pl.when(holder)
    def _():
        mirror_copy().start()
        for d in lines:
            x_copy(r_ref, d).start()
        r_local().start()

    for d in far_first:
        k_copy(d).wait_send()
    for d in far_first:
        q_copy(d).start()

    own_k.wait()
    for d in far_first:
        k_copy(d).wait_recv()
    for c in small:
        c.wait()
    gid = gid_ref[0]
    gid_y, gid_z = lax.rem(gid, ny), lax.div(gid, ny)

    def pick(parts, want):
        out = None
        for i, part in enumerate(parts):
            part = part.astype(F32) * jnp.where(want == i, 1.0, 0.0)
            out = part if out is None else out + part
        return out.astype(BF16)

    def z_dev(d):
        return (f, ((z + d) % nz) * ny + y)

    def z_copy(buf, ssem, rsem, d):
        return copy(buf.at[z], buf.at[z], ssem.at[d], rsem.at[d], z_dev(d))

    def k_ends():
        up = copy(kpad.at[pl.ds(rows, ROW)], kpad.at[pl.ds(0, ROW)], hks.at[0], hkr.at[0], z_dev(1))
        down = copy(kpad.at[pl.ds(ROW, ROW)], kpad.at[pl.ds(ROW + rows, ROW)], hks.at[1], hkr.at[1], z_dev(nz - 1))
        return up, down

    def v_ends():
        low, high = pl.ds(0, ROW), pl.ds(ROW, ROW)
        up = copy(vbuf.at[ny - 1, high], vend.at[low], hvs.at[0], hvr.at[0], z_dev(1))
        down = copy(vbuf.at[0, low], vend.at[high], hvs.at[1], hvr.at[1], z_dev(nz - 1))
        return up, down

    zk[z] = pick([kpad[ROW + b * BAND : ROW + (b + 1) * BAND, :] for b in range(ny)], gid_y)
    for d in range(1, nz):
        z_copy(zk, zks, zkr, d).start()
    for c in k_ends():
        c.start()

    q_gain = [qg_ref[pl.ds(y * hc + h, 1), :] for h in range(hc)]
    k_gain = [kg_ref[pl.ds(y * hc + h, 1), :] for h in range(hc)]
    knpad[:, :, HEAD:] = jnp.ones((hc, rows + 2 * ROW, HEAD), BF16)
    kng[:, :, HEAD:] = jnp.ones((hc, BAND, HEAD), BF16)

    def norm_rows(at, size):
        for h in range(hc):
            knpad[h, at, :HEAD] = normalize(kpad[at, h * HEAD : (h + 1) * HEAD], k_gain[h])

    def norm_band(b, carry):
        norm_rows(band_rows(b), BAND)
        return carry

    lax.fori_loop(0, ny, norm_band, 0)

    for d in far_first:
        q_copy(d).wait_send()
    for d in far_first:
        v_copy(d).start()

    for d in range(1, nz):
        z_copy(zk, zks, zkr, d).wait_recv()
    for c in k_ends():
        c.wait_recv()
    norm_rows(pl.ds(0, ROW), ROW)
    norm_rows(pl.ds(ROW + rows, ROW), ROW)
    kg_raw = pick([zk[i] for i in range(nz)], gid_z)
    for h in range(hc):
        kng[h, :, :HEAD] = normalize(kg_raw[:, h * HEAD : (h + 1) * HEAD], k_gain[h])

    @pl.when(relay)
    def _():
        mirror_copy().wait_recv()
        for d in lines:
            x_copy(rraw.at[mine], d).start()

    ones16 = jnp.ones((16, BAND), BF16)
    lane = lax.broadcasted_iota(jnp.int32, (BAND, WIN), 1)

    def band(b):
        low = jnp.where((z == 0) & (b == 0), ROW, 0)
        high = jnp.where((z == nz - 1) & (b == ny - 1), ROW + BAND, WIN)
        usable = (lane >= low) & (lane < high)
        window = pl.ds(pl.multiple_of(b * BAND, BAND), WIN)
        for h in range(hc):
            qn = normalize(qbuf[b, :, h * HEAD : (h + 1) * HEAD], q_gain[h])
            qn_s[b, h] = qn
            near = dot(qn, knpad[h, window, :HEAD], NT) * SCALE
            far = dot(qn, kng[h, :, :HEAD], NT) * SCALE
            near = jnp.where(usable, near, -1e30)
            top = jnp.maximum(jnp.max(near, -1, keepdims=True), jnp.max(far, -1, keepdims=True))
            near = jnp.exp(near - top)
            far = jnp.exp(far - top)
            total = jnp.sum(near, -1, keepdims=True) + jnp.sum(far, -1, keepdims=True)
            inv = 1.0 / total
            near = (near * inv).astype(BF16)
            far = (far * inv).astype(BF16)
            att[b, h, :, :WIN] = near
            att[b, h, :, WIN:] = far
            w_s[b, h, :, :WIN] = dot(ones16, near, NN)[:8]
            w_s[b, h, :, WIN:] = dot(ones16, far, NN)[:8]

    own_q.wait()
    for d in order:
        if d:
            q_copy(ny - d).wait_recv()
        band((y + d) % ny)

    half = lax.broadcasted_iota(jnp.int32, (1, HEAD), 1) < ROW
    given = []
    zw[z] = jnp.zeros((8, HEAD), F32)
    for h in range(hc):
        parts = [jnp.zeros((1, HEAD), F32) for _ in range(ny + 1)]
        far = jnp.zeros((1, HEAD), F32)
        for b in range(ny):
            parts[b] = parts[b] + w_s[b, h, 0:1, :HEAD]
            parts[b + 1] = parts[b + 1] + w_s[b, h, 0:1, HEAD:WIN]
            far = far + w_s[b, h, 0:1, WIN:]
        given.append(parts)
        zw[z, h : h + 1, :] = far
        zw[z, hc + h : hc + h + 1, :] = jnp.where(half, parts[0], parts[ny])
    for d in range(1, nz):
        z_copy(zw, zws, zwr, d).start()

    @pl.when(holder)
    def _():
        r_local().wait()

    if nf > 4:

        @pl.when(leaf)
        def _():
            mirror_copy().wait_recv()

    def twin_copy(at):
        return copy(rraw.at[at], rraw.at[at], fs, fr, (f + 1 - 2 * core, t))

    twin_copy(mine).start()

    e_acc[...] = jnp.zeros_like(e_acc)
    eg_acc[...] = jnp.zeros_like(eg_acc)

    def pulled(b, carry):
        window = pl.ds(pl.multiple_of(b * BAND, BAND), WIN)
        for h in range(hc):
            near = att[b, h, :, :WIN]
            far = att[b, h, :, WIN:]
            kn = knpad[h, window, :]
            kg = kng[h]
            mean_key = dot(near, kn, NN) + dot(far, kg, NN)
            qn = qn_s[b, h]
            qk = qn.astype(F32) * (mean_key[:, :HEAD] / mean_key[:, HEAD:])
            qk_high = qk.astype(BF16)
            qk_low = (qk - qk_high.astype(F32)).astype(BF16)
            right = jnp.concatenate([qn, qk_high, qk_low], 1)
            got = dot(near, right, TN)
            e_acc[h, window, :] += (
                kn[:, :HEAD].astype(F32) * got[:, :HEAD] - got[:, HEAD : 2 * HEAD] - got[:, 2 * HEAD :]
            )
            got = dot(far, right, TN)
            eg_acc[h] += kg[:, :HEAD].astype(F32) * got[:, :HEAD] - got[:, HEAD : 2 * HEAD] - got[:, 2 * HEAD :]
        return carry

    def pull_bands(first, last):
        lax.fori_loop(min(first, ny), min(last, ny), pulled, 0)

    pull_bands(0, 4)

    other = pl.ds(pl.multiple_of((1 - core) * shard, 64), shard)
    twin_copy(other).wait_recv()
    rpad[:, CLASSES // HEAD * HEAD :] = jnp.zeros((width, PAD - CLASSES // HEAD * HEAD), BF16)
    rpad[:, :CLASSES] = rraw[...]

    for d in range(1, nz):
        z_copy(zw, zws, zwr, d).wait_recv()
    below = zw[lax.rem(z + nz - 1, nz)]
    above = zw[lax.rem(z + 1, nz)]
    all_far = zw[0]
    for i in range(1, nz):
        all_far = all_far + zw[i]
    weights = []
    for h in range(hc):
        parts = given[h]
        parts[0] = parts[0] + below[hc + h : hc + h + 1]
        parts[ny] = parts[ny] + above[hc + h : hc + h + 1]
        own = []
        for b in range(ny):
            tile = jnp.concatenate([parts[b][:, ROW:], parts[b + 1][:, :ROW]], 1)
            own.append(tile + all_far[h : h + 1] * jnp.where(gid == z * ny + b, 1.0, 0.0))
        weights.append(split3(jnp.concatenate(own, 1)))

    def v_head(h):
        return vbuf[:, :, h * HEAD : (h + 1) * HEAD].reshape(rows, HEAD)

    own_v.wait()
    for d in far_first:
        v_copy(d).wait_recv()
    pooled = [jnp.sum(dot(weights[h], v_head(h), NN), 0, keepdims=True) for h in range(hc)]
    pooled = jnp.concatenate(pooled, 1) * (1.0 / tokens)
    logits = row_dot(pooled, rpad[...], NN)
    for i in range(8):
        lbuf[t, i : i + 1, :] = logits[:, i * HEAD : (i + 1) * HEAD]

    def exchange(buf, me, peers, ssem, rsem):
        def out(dev, number):
            return copy(buf.at[me], buf.at[me], ssem.at[number], rsem.at[me], dev)

        def come(slot, dev):
            return copy(buf.at[slot], buf.at[slot], ssem.at[0], rsem.at[slot], dev)

        def start():
            peers(lambda slot, dev, number: out(dev, number).start())

        def wait():
            peers(lambda slot, dev, number: come(slot, dev).wait_recv(), True)

        def wait_sent():
            peers(lambda slot, dev, number: out(dev, number).wait_send(), True)

        return start, wait, wait_sent

    def total_of(buf, n):
        out = buf[0]
        for i in range(1, n):
            out = out + buf[i]
        return out

    l_start, l_wait, l_sent = exchange(lbuf, t, t_peers, lsem, lrem)
    p_start, p_wait, p_sent = exchange(pbuf, f, f_peers, psem, prem)
    w_start, w_wait, w_sent = exchange(wbuf, f, f_peers, wsem, wrem)
    t_start, t_wait, t_sent = exchange(tbuf, t, t_peers, tsem, trem)
    l_start()

    for c in v_ends():
        c.start()
    zv[z] = pick([vbuf[b] for b in range(ny)], gid_y)
    for d in range(1, nz):
        z_copy(zv, zvs, zvr, d).start()
    pull_bands(4, 7)

    l_wait()
    logits = total_of(lbuf, nt)
    place = lax.broadcasted_iota(jnp.int32, (8, HEAD), 0) * HEAD + lax.broadcasted_iota(jnp.int32, (8, HEAD), 1)
    valid = place < CLASSES
    logits = jnp.where(valid, logits, -jnp.inf)

    def all_sum(x):
        return jnp.sum(jnp.sum(x, 0, keepdims=True), 1, keepdims=True)

    top = jnp.max(jnp.max(logits, 0, keepdims=True), 1, keepdims=True)
    probs = jnp.exp(logits - top)
    probs = probs / all_sum(probs)
    pbuf[f] = probs
    p_start()

    pull_bands(7, ny)
    for d in range(1, nz):
        z_copy(zv, zvs, zvr, d).wait_recv()
    for c in v_ends():
        c.wait_recv()
    vg = pick([zv[i] for i in range(nz)], gid_z)
    e_bf[...] = e_acc[...].astype(BF16)
    ones_rows = jnp.ones((16, rows), BF16)
    for h in range(hc):
        cols = slice(h * HEAD, (h + 1) * HEAD)
        eg = eg_acc[h].astype(BF16)
        v = v_head(h)
        m = dot(v, e_bf[h, ROW : ROW + rows, :], TN) + dot(vg[:, cols], eg, TN)
        m = m + dot(vend[:ROW, cols], e_bf[h, :ROW, :], TN)
        m = m + dot(vend[ROW:, cols], e_bf[h, ROW + rows :, :], TN)
        middle = dot(v, ones_rows, (((0,), (1,)), ((), ())))[:, :1] * (1.0 / rows)
        total = jnp.sum(e_bf[h].astype(F32), 0, keepdims=True) + jnp.sum(eg.astype(F32), 0, keepdims=True)
        m = m - middle * total
        high = m.astype(BF16)
        pull[h, :, :HEAD] = high
        pull[h, :, HEAD:] = (m - high.astype(F32)).astype(BF16)

    p_wait()
    mean = total_of(pbuf, nf) * (1.0 / nf)
    log_mean = jnp.where(valid, jnp.log(mean), 0.0)
    entropy = -all_sum(jnp.where(valid, mean * log_mean, 0.0))
    ent_ref[...] = jnp.broadcast_to(entropy, ent_ref.shape)
    upstream = jnp.where(valid, -(log_mean + 1.0) * (1.0 / nf), 0.0)
    dlogits = probs * (upstream - all_sum(probs * upstream))
    dlogits = jnp.concatenate([dlogits[i : i + 1] for i in range(8)], 1)
    dpooled = row_dot(dlogits, rpad[...], NT) * (1.0 / tokens)
    wbuf[f] = jnp.zeros((8, HEAD), F32)
    for h in range(hc):
        cols = slice(h * HEAD, (h + 1) * HEAD)
        got = row_dot(dpooled[:, cols], pull[h], NN)
        wbuf[f, h : h + 1, :] = (got[:, :HEAD] + got[:, HEAD:]) * SCALE
    w_start()
    w_wait()
    tbuf[t] = total_of(wbuf, nf)
    t_start()

    for d in far_first:
        v_copy(d).wait_send()
    for d in range(1, nz):
        z_copy(zk, zks, zkr, d).wait_send()
        z_copy(zv, zvs, zvr, d).wait_send()
        z_copy(zw, zws, zwr, d).wait_send()
    for c in k_ends() + v_ends():
        c.wait_send()

    @pl.when(holder)
    def _():
        mirror_copy().wait_send()
        for d in lines:
            x_copy(r_ref, d).wait_send()

    @pl.when(relay)
    def _():
        for d in lines:
            x_copy(rraw.at[mine], d).wait_send()

    twin_copy(mine).wait_send()
    l_sent()
    p_sent()
    w_sent()
    t_sent()
    t_wait()
    for i in range(ny):
        got = None
        for j in range(nz):
            row = jnp.where(chip % 2 == 0, j, nz - 1 - j)
            part = tbuf[row * ny + i]
            got = part if got is None else got + part
        w_out[i * hc : (i + 1) * hc, :] = got[:hc]


def make_body(ny):
    def body(queries, keys, values, readout, global_block, q_gain, k_gain):
        nf, nt = lax.axis_size("fsdp"), lax.axis_size("tok")
        nz = nt // ny
        heads = q_gain.shape[0] // HEAD
        hc = heads // ny
        width = hc * HEAD
        rows = ny * BAND
        padded = rows + 2 * ROW
        tokens = nt * BAND
        dma = pltpu.SemaphoreType.DMA
        vmem = pltpu.VMEM
        scratch = [
            pltpu.SMEM((1,), jnp.int32),
            vmem((heads, HEAD), F32),
            vmem((heads, HEAD), F32),
            vmem((padded, width), BF16),
            vmem((ny, BAND, width), BF16),
            vmem((2 * ROW, width), BF16),
            vmem((ny, BAND, width), BF16),
            vmem((hc, padded, 2 * HEAD), BF16),
            vmem((hc, BAND, 2 * HEAD), BF16),
            vmem((nz, BAND, width), BF16),
            vmem((nz, BAND, width), BF16),
            vmem((nz, 8, HEAD), F32),
            vmem((width, CLASSES), BF16),
            vmem((width, PAD), BF16),
            vmem((ny, hc, BAND, SEEN), BF16),
            vmem((ny, hc, BAND, HEAD), BF16),
            vmem((ny, hc, 8, SEEN), F32),
            vmem((hc, padded, HEAD), F32),
            vmem((hc, BAND, HEAD), F32),
            vmem((hc, padded, HEAD), BF16),
            vmem((hc, HEAD, 2 * HEAD), BF16),
            vmem((nt, 8, HEAD), F32),
            vmem((nf, 8, HEAD), F32),
            vmem((nf, 8, HEAD), F32),
            vmem((nt, 8, HEAD), F32),
        ]
        scratch += [dma((ny,))] * 6 + [dma((7,))] + [dma((nz,))] * 4 + [dma((2,))] * 4 + [dma((nz,))] * 2
        scratch += [dma((nf // 4,)), dma((1,)), dma, dma]
        scratch += [dma((nt,))] * 2 + [dma((nf,))] * 4 + [dma((nt,))] * 2
        hbm = pl.BlockSpec(memory_space=pl.ANY)
        in_hbm = pl.BlockSpec(memory_space=pltpu.HBM)
        whole = pl.BlockSpec(memory_space=pltpu.VMEM)
        entropy, total = pl.pallas_call(
            functools.partial(kernel, ny, nz, nf, hc, tokens),
            out_shape=(
                jax.ShapeDtypeStruct((8, HEAD), F32),
                jax.ShapeDtypeStruct((heads, HEAD), F32),
            ),
            in_specs=[in_hbm, hbm, hbm, hbm, hbm, in_hbm, in_hbm],
            out_specs=(whole, whole),
            scratch_shapes=scratch,
            compiler_params=pltpu.CompilerParams(
                collective_id=0, has_side_effects=True, vmem_limit_bytes=60 * 2**20
            ),
            name="adapt",
        )(
            global_block,
            queries,
            keys,
            values,
            readout,
            q_gain.reshape(heads, HEAD),
            k_gain.reshape(heads, HEAD),
        )
        total = total.reshape(-1)
        return entropy[0, 0], total / q_gain, total / k_gain

    return body


def solution(mesh):
    in_specs = (
        P("fsdp", "tok", None),
        P("fsdp", "tok", None),
        P("fsdp", "tok", None),
        P("fsdp", None),
        P("fsdp"),
        P(),
        P(),
    )
    out_specs = (P(), P(), P())
    return jax.shard_map(make_body(Y), mesh=mesh, in_specs=in_specs, out_specs=out_specs, check_vma=False)
```

```python
import functools

import jax
import jax.numpy as jnp
from jax import lax
from jax.experimental import pallas as pl
from jax.experimental.pallas import tpu as pltpu
from jax.sharding import PartitionSpec as P

HEAD = 128
ROW = 64
BAND = 128
CLASSES = 1000
PAD = 1024
WIN = BAND + 2 * ROW
SEEN = WIN + BAND
Y = 8
MESH = pl.DeviceIdType.MESH
F32 = jnp.float32
BF16 = jnp.bfloat16
NT = (((1,), (1,)), ((), ()))
NN = (((1,), (0,)), ((), ()))
TN = (((0,), (0,)), ((), ()))
SCALE = HEAD**-0.5


def dot(a, b, dims):
    return lax.dot_general(a, b, dims, preferred_element_type=F32)


def normalize(x, gain):
    x = x.astype(F32)
    x = x - jnp.mean(x, -1, keepdims=True)
    var = jnp.mean(x * x, -1, keepdims=True)
    return (x * lax.rsqrt(var + 1e-06) * gain).astype(BF16)


def split3(x):
    x = jnp.broadcast_to(x, (16, x.shape[1]))
    high = x.astype(BF16).astype(F32)
    rest = x - high
    mid = rest.astype(BF16).astype(F32)
    low = rest - mid
    row = lax.broadcasted_iota(jnp.int32, x.shape, 0)
    out = jnp.where(row == 0, high, jnp.where(row == 1, mid, jnp.where(row == 2, low, 0.0)))
    return out.astype(BF16)


def row_dot(x, b, dims):
    return jnp.sum(dot(split3(x), b, dims), 0, keepdims=True)


def kernel(
    ny, nz, nf, hc, tokens,
    gid_hbm, q_ref, k_ref, v_ref, r_ref, qg_hbm, kg_hbm,
    ent_ref, w_out,
    gid_ref, qg_ref, kg_ref,
    kpad, vbuf, vend, qbuf, knpad, kng, zk, zv, zw, rraw, rpad, att, qn_s, w_s, e_acc, eg_acc, e_bf, pull,
    lbuf, pbuf, wbuf, tbuf,
    ks, kr, vs, vr, qs, qr, local, zks, zkr, zvs, zvr, hks, hkr, hvs, hvr, zws, zwr,
    rs, rr, fs, fr, lsem, lrem, psem, prem, wsem, wrem, tsem, trem,
):
    nt = nz * ny
    f, t = lax.axis_index("fsdp"), lax.axis_index("tok")
    z, y = t // ny, t % ny
    core = f % 2
    width = hc * HEAD
    rows = ny * BAND
    shard = r_ref.shape[0]

    def copy(src, dst, ssem, rsem, dev):
        return pltpu.make_async_remote_copy(
            src_ref=src, dst_ref=dst, send_sem=ssem, recv_sem=rsem, device_id=dev, device_id_type=MESH
        )

    def chunk(c):
        return pl.ds(pl.multiple_of(c * width, HEAD), width)

    def band_rows(b):
        return pl.ds(pl.multiple_of(ROW + b * BAND, ROW), BAND)

    own_k = pltpu.make_async_copy(k_ref.at[0, :, chunk(y)], kpad.at[band_rows(y)], local.at[0])
    own_v = pltpu.make_async_copy(v_ref.at[0, :, chunk(y)], vbuf.at[y], local.at[1])
    own_q = pltpu.make_async_copy(q_ref.at[0, :, chunk(y)], qbuf.at[y], local.at[2])
    own_k.start()
    own_v.start()
    own_q.start()

    small = [
        pltpu.make_async_copy(gid_hbm, gid_ref, local.at[4]),
        pltpu.make_async_copy(qg_hbm, qg_ref, local.at[5]),
        pltpu.make_async_copy(kg_hbm, kg_ref, local.at[6]),
    ]
    for c in small:
        c.start()

    chip = f // 2
    mirror_t = (nz - 1 - z) * ny + y

    def wrap(i, n):
        return jnp.where(i >= n, i - n, i)

    def f_dev(p):
        return (p, jnp.where((p // 2) % 2 == chip % 2, t, mirror_t))

    def t_peers(act, far_last=False):
        def column(k, carry):
            if far_last:
                k = ny - 2 - k
            d = jnp.where(k % 2 == 1, ny // 2 - (k + 1) // 2, ny // 2 + k // 2)
            far_y = wrap(y + d, ny)
            for i in range(nz):
                p = wrap(z + i, nz) * ny + far_y
                act(p, (f, p), i * ny + d)
            return carry

        def own_column():
            for i in range(1, nz):
                p = wrap(z + i, nz) * ny + y
                act(p, (f, p), i * ny)

        if far_last:
            own_column()
        lax.fori_loop(0, ny - 1, column, 0)
        if not far_last:
            own_column()

    def f_peers(act, far_last=False):
        nx = nf // 4
        x = f // 4
        steps = sorted(range(1, nf), key=lambda s: -(2 * min(s // 4, nx - s // 4) + 3 * (s // 2 % 2)))
        for s in steps[::-1] if far_last else steps:
            other = chip % 2
            if s // 2 % 2:
                other = 1 - other
            twin = 1 - core if s % 2 else core
            p = (wrap(x + s // 4, nx) * 2 + other) * 2 + twin
            act(p, f_dev(p), s)

    barrier = pltpu.get_barrier_semaphore()

    def greet(dev):
        pl.semaphore_signal(barrier, inc=1, device_id=dev, device_id_type=MESH)

    t_peers(lambda slot, dev, number: greet(dev))
    f_peers(lambda slot, dev, number: greet(dev))
    pl.semaphore_wait(barrier, nt - 1 + nf - 1)

    order = [0]
    for d in range(1, ny // 2 + 1):
        order.append(d)
        if ny - d != d:
            order.append(ny - d)

    def y_dev(d):
        return (f, z * ny + (y + d) % ny)

    def k_copy(d):
        p = (y + d) % ny
        return copy(k_ref.at[0, :, chunk(p)], kpad.at[band_rows(y)], ks.at[d], kr.at[d], y_dev(d))

    def v_copy(d):
        p = (y + d) % ny
        return copy(v_ref.at[0, :, chunk(p)], vbuf.at[y], vs.at[d], vr.at[d], y_dev(d))

    def q_copy(d):
        p = (y + d) % ny
        return copy(q_ref.at[0, :, chunk(p)], qbuf.at[y], qs.at[d], qr.at[d], y_dev(d))

    others = order[1:]
    for d in others:
        k_copy(d).start()

    mine = pl.ds(pl.multiple_of(core * shard, 64), shard)
    holder = chip == y
    relay = (chip // 2 == y // 2) & (chip != y)
    leaf = chip // 2 != y // 2
    lines = range(1, nf // 4)

    def x_copy(src, d):
        return copy(src, rraw.at[mine], rs.at[d], rr.at[0], ((f + 4 * d) % nf, t))

    def mirror_copy():
        return copy(r_ref, rraw.at[mine], rs.at[0], rr.at[0], f_dev(f + 2 - 4 * (chip % 2)))

    def r_local():
        return pltpu.make_async_copy(r_ref, rraw.at[mine], local.at[3])

    @pl.when(holder)
    def _():
        mirror_copy().start()
        for d in lines:
            x_copy(r_ref, d).start()
        r_local().start()

    for d in others:
        k_copy(d).wait_send()
    for d in others:
        q_copy(d).start()

    own_k.wait()
    for d in others:
        k_copy(d).wait_recv()
    for c in small:
        c.wait()
    gid = gid_ref[0]
    gid_y, gid_z = lax.rem(gid, ny), lax.div(gid, ny)

    def pick(parts, want):
        out = None
        for i, part in enumerate(parts):
            part = part.astype(F32) * jnp.where(want == i, 1.0, 0.0)
            out = part if out is None else out + part
        return out.astype(BF16)

    def z_dev(d):
        return (f, ((z + d) % nz) * ny + y)

    def z_copy(buf, ssem, rsem, d):
        return copy(buf.at[z], buf.at[z], ssem.at[d], rsem.at[d], z_dev(d))

    def k_ends():
        up = copy(kpad.at[pl.ds(rows, ROW)], kpad.at[pl.ds(0, ROW)], hks.at[0], hkr.at[0], z_dev(1))
        down = copy(kpad.at[pl.ds(ROW, ROW)], kpad.at[pl.ds(ROW + rows, ROW)], hks.at[1], hkr.at[1], z_dev(nz - 1))
        return up, down

    def v_ends():
        low, high = pl.ds(0, ROW), pl.ds(ROW, ROW)
        up = copy(vbuf.at[ny - 1, high], vend.at[low], hvs.at[0], hvr.at[0], z_dev(1))
        down = copy(vbuf.at[0, low], vend.at[high], hvs.at[1], hvr.at[1], z_dev(nz - 1))
        return up, down

    zk[z] = pick([kpad[ROW + b * BAND : ROW + (b + 1) * BAND, :] for b in range(ny)], gid_y)
    for d in range(1, nz):
        z_copy(zk, zks, zkr, d).start()
    for c in k_ends():
        c.start()

    q_gain = [qg_ref[pl.ds(y * hc + h, 1), :] for h in range(hc)]
    k_gain = [kg_ref[pl.ds(y * hc + h, 1), :] for h in range(hc)]
    knpad[:, :, HEAD:] = jnp.ones((hc, rows + 2 * ROW, HEAD), BF16)
    kng[:, :, HEAD:] = jnp.ones((hc, BAND, HEAD), BF16)

    def norm_rows(at, size):
        for h in range(hc):
            knpad[h, at, :HEAD] = normalize(kpad[at, h * HEAD : (h + 1) * HEAD], k_gain[h])

    def norm_band(b, carry):
        norm_rows(band_rows(b), BAND)
        return carry

    lax.fori_loop(0, ny, norm_band, 0)

    for d in others:
        q_copy(d).wait_send()
    for d in others:
        v_copy(d).start()

    for d in range(1, nz):
        z_copy(zk, zks, zkr, d).wait_recv()
    for c in k_ends():
        c.wait_recv()
    norm_rows(pl.ds(0, ROW), ROW)
    norm_rows(pl.ds(ROW + rows, ROW), ROW)
    kg_raw = pick([zk[i] for i in range(nz)], gid_z)
    for h in range(hc):
        kng[h, :, :HEAD] = normalize(kg_raw[:, h * HEAD : (h + 1) * HEAD], k_gain[h])

    @pl.when(relay)
    def _():
        mirror_copy().wait_recv()
        for d in lines:
            x_copy(rraw.at[mine], d).start()

    ones16 = jnp.ones((16, BAND), BF16)
    lane = lax.broadcasted_iota(jnp.int32, (BAND, WIN), 1)

    def band(b):
        low = jnp.where((z == 0) & (b == 0), ROW, 0)
        high = jnp.where((z == nz - 1) & (b == ny - 1), ROW + BAND, WIN)
        usable = (lane >= low) & (lane < high)
        window = pl.ds(pl.multiple_of(b * BAND, BAND), WIN)
        for h in range(hc):
            qn = normalize(qbuf[b, :, h * HEAD : (h + 1) * HEAD], q_gain[h])
            qn_s[b, h] = qn
            near = dot(qn, knpad[h, window, :HEAD], NT) * SCALE
            far = dot(qn, kng[h, :, :HEAD], NT) * SCALE
            near = jnp.where(usable, near, -1e30)
            top = jnp.maximum(jnp.max(near, -1, keepdims=True), jnp.max(far, -1, keepdims=True))
            near = jnp.exp(near - top)
            far = jnp.exp(far - top)
            total = jnp.sum(near, -1, keepdims=True) + jnp.sum(far, -1, keepdims=True)
            inv = 1.0 / total
            near = (near * inv).astype(BF16)
            far = (far * inv).astype(BF16)
            att[b, h, :, :WIN] = near
            att[b, h, :, WIN:] = far
            w_s[b, h, :, :WIN] = dot(ones16, near, NN)[:8]
            w_s[b, h, :, WIN:] = dot(ones16, far, NN)[:8]

    own_q.wait()
    for d in order:
        if d:
            q_copy(ny - d).wait_recv()
        band((y + d) % ny)

    half = lax.broadcasted_iota(jnp.int32, (1, HEAD), 1) < ROW
    given = []
    zw[z] = jnp.zeros((8, HEAD), F32)
    for h in range(hc):
        parts = [jnp.zeros((1, HEAD), F32) for _ in range(ny + 1)]
        far = jnp.zeros((1, HEAD), F32)
        for b in range(ny):
            parts[b] = parts[b] + w_s[b, h, 0:1, :HEAD]
            parts[b + 1] = parts[b + 1] + w_s[b, h, 0:1, HEAD:WIN]
            far = far + w_s[b, h, 0:1, WIN:]
        given.append(parts)
        zw[z, h : h + 1, :] = far
        zw[z, hc + h : hc + h + 1, :] = jnp.where(half, parts[0], parts[ny])
    for d in range(1, nz):
        z_copy(zw, zws, zwr, d).start()

    @pl.when(holder)
    def _():
        r_local().wait()

    if nf > 4:

        @pl.when(leaf)
        def _():
            mirror_copy().wait_recv()

    def twin_copy(at):
        return copy(rraw.at[at], rraw.at[at], fs, fr, (f + 1 - 2 * core, t))

    twin_copy(mine).start()

    e_acc[...] = jnp.zeros_like(e_acc)
    eg_acc[...] = jnp.zeros_like(eg_acc)

    def pulled(b, carry):
        window = pl.ds(pl.multiple_of(b * BAND, BAND), WIN)
        for h in range(hc):
            near = att[b, h, :, :WIN]
            far = att[b, h, :, WIN:]
            kn = knpad[h, window, :]
            kg = kng[h]
            mean_key = dot(near, kn, NN) + dot(far, kg, NN)
            qn = qn_s[b, h]
            qk = qn.astype(F32) * (mean_key[:, :HEAD] / mean_key[:, HEAD:])
            qk_high = qk.astype(BF16)
            qk_low = (qk - qk_high.astype(F32)).astype(BF16)
            right = jnp.concatenate([qn, qk_high, qk_low], 1)
            got = dot(near, right, TN)
            e_acc[h, window, :] += (
                kn[:, :HEAD].astype(F32) * got[:, :HEAD] - got[:, HEAD : 2 * HEAD] - got[:, 2 * HEAD :]
            )
            got = dot(far, right, TN)
            eg_acc[h] += kg[:, :HEAD].astype(F32) * got[:, :HEAD] - got[:, HEAD : 2 * HEAD] - got[:, 2 * HEAD :]
        return carry

    def pull_bands(first, last):
        lax.fori_loop(min(first, ny), min(last, ny), pulled, 0)

    pull_bands(0, 4)

    other = pl.ds(pl.multiple_of((1 - core) * shard, 64), shard)
    twin_copy(other).wait_recv()
    rpad[:, CLASSES // HEAD * HEAD :] = jnp.zeros((width, PAD - CLASSES // HEAD * HEAD), BF16)
    rpad[:, :CLASSES] = rraw[...]

    for d in range(1, nz):
        z_copy(zw, zws, zwr, d).wait_recv()
    below = zw[lax.rem(z + nz - 1, nz)]
    above = zw[lax.rem(z + 1, nz)]
    all_far = zw[0]
    for i in range(1, nz):
        all_far = all_far + zw[i]
    weights = []
    for h in range(hc):
        parts = given[h]
        parts[0] = parts[0] + below[hc + h : hc + h + 1]
        parts[ny] = parts[ny] + above[hc + h : hc + h + 1]
        own = []
        for b in range(ny):
            tile = jnp.concatenate([parts[b][:, ROW:], parts[b + 1][:, :ROW]], 1)
            own.append(tile + all_far[h : h + 1] * jnp.where(gid == z * ny + b, 1.0, 0.0))
        weights.append(split3(jnp.concatenate(own, 1)))

    def v_head(h):
        return vbuf[:, :, h * HEAD : (h + 1) * HEAD].reshape(rows, HEAD)

    own_v.wait()
    for d in others:
        v_copy(d).wait_recv()
    pooled = [jnp.sum(dot(weights[h], v_head(h), NN), 0, keepdims=True) for h in range(hc)]
    pooled = jnp.concatenate(pooled, 1) * (1.0 / tokens)
    logits = row_dot(pooled, rpad[...], NN)
    for i in range(8):
        lbuf[t, i : i + 1, :] = logits[:, i * HEAD : (i + 1) * HEAD]

    def exchange(buf, me, peers, ssem, rsem):
        def out(dev, number):
            return copy(buf.at[me], buf.at[me], ssem.at[number], rsem.at[me], dev)

        def come(slot, dev):
            return copy(buf.at[slot], buf.at[slot], ssem.at[0], rsem.at[slot], dev)

        def start():
            peers(lambda slot, dev, number: out(dev, number).start())

        def wait():
            peers(lambda slot, dev, number: come(slot, dev).wait_recv(), True)

        def wait_sent():
            peers(lambda slot, dev, number: out(dev, number).wait_send(), True)

        return start, wait, wait_sent

    def total_of(buf, n):
        out = buf[0]
        for i in range(1, n):
            out = out + buf[i]
        return out

    l_start, l_wait, l_sent = exchange(lbuf, t, t_peers, lsem, lrem)
    p_start, p_wait, p_sent = exchange(pbuf, f, f_peers, psem, prem)
    w_start, w_wait, w_sent = exchange(wbuf, f, f_peers, wsem, wrem)
    t_start, t_wait, t_sent = exchange(tbuf, t, t_peers, tsem, trem)
    l_start()

    for c in v_ends():
        c.start()
    zv[z] = pick([vbuf[b] for b in range(ny)], gid_y)
    for d in range(1, nz):
        z_copy(zv, zvs, zvr, d).start()
    pull_bands(4, 7)

    l_wait()
    logits = total_of(lbuf, nt)
    place = lax.broadcasted_iota(jnp.int32, (8, HEAD), 0) * HEAD + lax.broadcasted_iota(jnp.int32, (8, HEAD), 1)
    valid = place < CLASSES
    logits = jnp.where(valid, logits, -jnp.inf)

    def all_sum(x):
        return jnp.sum(jnp.sum(x, 0, keepdims=True), 1, keepdims=True)

    top = jnp.max(jnp.max(logits, 0, keepdims=True), 1, keepdims=True)
    probs = jnp.exp(logits - top)
    probs = probs / all_sum(probs)
    pbuf[f] = probs
    p_start()

    pull_bands(7, ny)
    for d in range(1, nz):
        z_copy(zv, zvs, zvr, d).wait_recv()
    for c in v_ends():
        c.wait_recv()
    vg = pick([zv[i] for i in range(nz)], gid_z)
    e_bf[...] = e_acc[...].astype(BF16)
    ones_rows = jnp.ones((16, rows), BF16)
    for h in range(hc):
        cols = slice(h * HEAD, (h + 1) * HEAD)
        eg = eg_acc[h].astype(BF16)
        v = v_head(h)
        m = dot(v, e_bf[h, ROW : ROW + rows, :], TN) + dot(vg[:, cols], eg, TN)
        m = m + dot(vend[:ROW, cols], e_bf[h, :ROW, :], TN)
        m = m + dot(vend[ROW:, cols], e_bf[h, ROW + rows :, :], TN)
        middle = dot(v, ones_rows, (((0,), (1,)), ((), ())))[:, :1] * (1.0 / rows)
        total = jnp.sum(e_bf[h].astype(F32), 0, keepdims=True) + jnp.sum(eg.astype(F32), 0, keepdims=True)
        m = m - middle * total
        high = m.astype(BF16)
        pull[h, :, :HEAD] = high
        pull[h, :, HEAD:] = (m - high.astype(F32)).astype(BF16)

    p_wait()
    mean = total_of(pbuf, nf) * (1.0 / nf)
    log_mean = jnp.where(valid, jnp.log(mean), 0.0)
    entropy = -all_sum(jnp.where(valid, mean * log_mean, 0.0))
    ent_ref[...] = jnp.broadcast_to(entropy, ent_ref.shape)
    upstream = jnp.where(valid, -(log_mean + 1.0) * (1.0 / nf), 0.0)
    dlogits = probs * (upstream - all_sum(probs * upstream))
    dlogits = jnp.concatenate([dlogits[i : i + 1] for i in range(8)], 1)
    dpooled = row_dot(dlogits, rpad[...], NT) * (1.0 / tokens)
    wbuf[f] = jnp.zeros((8, HEAD), F32)
    for h in range(hc):
        cols = slice(h * HEAD, (h + 1) * HEAD)
        got = row_dot(dpooled[:, cols], pull[h], NN)
        wbuf[f, h : h + 1, :] = (got[:, :HEAD] + got[:, HEAD:]) * SCALE
    w_start()
    w_wait()
    tbuf[t] = total_of(wbuf, nf)
    t_start()

    for d in others:
        v_copy(d).wait_send()
    for d in range(1, nz):
        z_copy(zk, zks, zkr, d).wait_send()
        z_copy(zv, zvs, zvr, d).wait_send()
        z_copy(zw, zws, zwr, d).wait_send()
    for c in k_ends() + v_ends():
        c.wait_send()

    @pl.when(holder)
    def _():
        mirror_copy().wait_send()
        for d in lines:
            x_copy(r_ref, d).wait_send()

    @pl.when(relay)
    def _():
        for d in lines:
            x_copy(rraw.at[mine], d).wait_send()

    twin_copy(mine).wait_send()
    l_sent()
    p_sent()
    w_sent()
    t_sent()
    t_wait()
    for i in range(ny):
        got = None
        for j in range(nz):
            row = jnp.where(chip % 2 == 0, j, nz - 1 - j)
            part = tbuf[row * ny + i]
            got = part if got is None else got + part
        w_out[i * hc : (i + 1) * hc, :] = got[:hc]


def make_body(ny):
    def body(queries, keys, values, readout, global_block, q_gain, k_gain):
        nf, nt = lax.axis_size("fsdp"), lax.axis_size("tok")
        nz = nt // ny
        heads = q_gain.shape[0] // HEAD
        hc = heads // ny
        width = hc * HEAD
        rows = ny * BAND
        padded = rows + 2 * ROW
        tokens = nt * BAND
        dma = pltpu.SemaphoreType.DMA
        vmem = pltpu.VMEM
        scratch = [
            pltpu.SMEM((1,), jnp.int32),
            vmem((heads, HEAD), F32),
            vmem((heads, HEAD), F32),
            vmem((padded, width), BF16),
            vmem((ny, BAND, width), BF16),
            vmem((2 * ROW, width), BF16),
            vmem((ny, BAND, width), BF16),
            vmem((hc, padded, 2 * HEAD), BF16),
            vmem((hc, BAND, 2 * HEAD), BF16),
            vmem((nz, BAND, width), BF16),
            vmem((nz, BAND, width), BF16),
            vmem((nz, 8, HEAD), F32),
            vmem((width, CLASSES), BF16),
            vmem((width, PAD), BF16),
            vmem((ny, hc, BAND, SEEN), BF16),
            vmem((ny, hc, BAND, HEAD), BF16),
            vmem((ny, hc, 8, SEEN), F32),
            vmem((hc, padded, HEAD), F32),
            vmem((hc, BAND, HEAD), F32),
            vmem((hc, padded, HEAD), BF16),
            vmem((hc, HEAD, 2 * HEAD), BF16),
            vmem((nt, 8, HEAD), F32),
            vmem((nf, 8, HEAD), F32),
            vmem((nf, 8, HEAD), F32),
            vmem((nt, 8, HEAD), F32),
        ]
        scratch += [dma((ny,))] * 6 + [dma((7,))] + [dma((nz,))] * 4 + [dma((2,))] * 4 + [dma((nz,))] * 2
        scratch += [dma((nf // 4,)), dma((1,)), dma, dma]
        scratch += [dma((nt,))] * 2 + [dma((nf,))] * 4 + [dma((nt,))] * 2
        hbm = pl.BlockSpec(memory_space=pl.ANY)
        in_hbm = pl.BlockSpec(memory_space=pltpu.HBM)
        whole = pl.BlockSpec(memory_space=pltpu.VMEM)
        entropy, total = pl.pallas_call(
            functools.partial(kernel, ny, nz, nf, hc, tokens),
            out_shape=(
                jax.ShapeDtypeStruct((8, HEAD), F32),
                jax.ShapeDtypeStruct((heads, HEAD), F32),
            ),
            in_specs=[in_hbm, hbm, hbm, hbm, hbm, in_hbm, in_hbm],
            out_specs=(whole, whole),
            scratch_shapes=scratch,
            compiler_params=pltpu.CompilerParams(
                collective_id=0, has_side_effects=True, vmem_limit_bytes=60 * 2**20
            ),
            name="adapt",
        )(
            global_block,
            queries,
            keys,
            values,
            readout,
            q_gain.reshape(heads, HEAD),
            k_gain.reshape(heads, HEAD),
        )
        total = total.reshape(-1)
        return entropy[0, 0], total / q_gain, total / k_gain

    return body


def solution(mesh):
    in_specs = (
        P("fsdp", "tok", None),
        P("fsdp", "tok", None),
        P("fsdp", "tok", None),
        P("fsdp", None),
        P("fsdp"),
        P(),
        P(),
    )
    out_specs = (P(), P(), P())
    return jax.shard_map(make_body(Y), mesh=mesh, in_specs=in_specs, out_specs=out_specs, check_vma=False)
```

```python
import functools

import jax
import jax.numpy as jnp
from jax import lax
from jax.experimental import pallas as pl
from jax.experimental.pallas import tpu as pltpu
from jax.sharding import PartitionSpec as P

HEAD = 128
ROW = 64
BAND = 128
CLASSES = 1000
PAD = 1024
WIN = BAND + 2 * ROW
SEEN = WIN + BAND
Y = 8
MESH = pl.DeviceIdType.MESH
F32 = jnp.float32
BF16 = jnp.bfloat16
NT = (((1,), (1,)), ((), ()))
NN = (((1,), (0,)), ((), ()))
TN = (((0,), (0,)), ((), ()))
SCALE = HEAD**-0.5


def dot(a, b, dims):
    return lax.dot_general(a, b, dims, preferred_element_type=F32)


def normalize(x, gain):
    x = x.astype(F32)
    x = x - jnp.mean(x, -1, keepdims=True)
    var = jnp.mean(x * x, -1, keepdims=True)
    return (x * lax.rsqrt(var + 1e-06) * gain).astype(BF16)


def split3(x):
    x = jnp.broadcast_to(x, (16, x.shape[1]))
    high = x.astype(BF16).astype(F32)
    rest = x - high
    mid = rest.astype(BF16).astype(F32)
    low = rest - mid
    row = lax.broadcasted_iota(jnp.int32, x.shape, 0)
    out = jnp.where(row == 0, high, jnp.where(row == 1, mid, jnp.where(row == 2, low, 0.0)))
    return out.astype(BF16)


def row_dot(x, b, dims):
    return jnp.sum(dot(split3(x), b, dims), 0, keepdims=True)


def kernel(
    ny, nz, nf, hc, tokens,
    gid_hbm, q_ref, k_ref, v_ref, r_ref, qg_hbm, kg_hbm,
    ent_ref, w_out,
    gid_ref, qg_ref, kg_ref,
    kpad, vbuf, vend, qbuf, knpad, kng, zk, zv, zw, rraw, rpad, att, qn_s, w_s, e_acc, eg_acc, e_bf, pull,
    lbuf, pbuf, wbuf, tbuf,
    ks, kr, vs, vr, qs, qr, local, zks, zkr, zvs, zvr, hks, hkr, hvs, hvr, zws, zwr,
    rs, rr, fs, fr, lsem, lrem, psem, prem, wsem, wrem, tsem, trem,
):
    nt = nz * ny
    f, t = lax.axis_index("fsdp"), lax.axis_index("tok")
    z, y = t // ny, t % ny
    core = f % 2
    width = hc * HEAD
    rows = ny * BAND
    shard = r_ref.shape[0]

    def copy(src, dst, ssem, rsem, dev):
        return pltpu.make_async_remote_copy(
            src_ref=src, dst_ref=dst, send_sem=ssem, recv_sem=rsem, device_id=dev, device_id_type=MESH
        )

    def chunk(c):
        return pl.ds(pl.multiple_of(c * width, HEAD), width)

    def band_rows(b):
        return pl.ds(pl.multiple_of(ROW + b * BAND, ROW), BAND)

    own_k = pltpu.make_async_copy(k_ref.at[0, :, chunk(y)], kpad.at[band_rows(y)], local.at[0])
    own_v = pltpu.make_async_copy(v_ref.at[0, :, chunk(y)], vbuf.at[y], local.at[1])
    own_q = pltpu.make_async_copy(q_ref.at[0, :, chunk(y)], qbuf.at[y], local.at[2])
    own_k.start()
    own_v.start()
    own_q.start()

    small = [
        pltpu.make_async_copy(gid_hbm, gid_ref, local.at[4]),
        pltpu.make_async_copy(qg_hbm, qg_ref, local.at[5]),
        pltpu.make_async_copy(kg_hbm, kg_ref, local.at[6]),
    ]
    for c in small:
        c.start()

    chip = f // 2
    mirror_t = (nz - 1 - z) * ny + y

    def wrap(i, n):
        return jnp.where(i >= n, i - n, i)

    def f_dev(p):
        return (p, jnp.where((p // 2) % 2 == chip % 2, t, mirror_t))

    def t_peers(act, far_last=False):
        def column(k, carry):
            if far_last:
                k = ny - 2 - k
            d = jnp.where(k % 2 == 1, ny // 2 - (k + 1) // 2, ny // 2 + k // 2)
            far_y = wrap(y + d, ny)
            for i in range(nz):
                p = wrap(z + i, nz) * ny + far_y
                act(p, (f, p), i * ny + d)
            return carry

        def own_column():
            for i in range(1, nz):
                p = wrap(z + i, nz) * ny + y
                act(p, (f, p), i * ny)

        if far_last:
            own_column()
        lax.fori_loop(0, ny - 1, column, 0)
        if not far_last:
            own_column()

    def f_peers(act, far_last=False):
        nx = nf // 4
        x = f // 4
        steps = sorted(range(1, nf), key=lambda s: -(2 * min(s // 4, nx - s // 4) + 3 * (s // 2 % 2)))
        for s in steps[::-1] if far_last else steps:
            other = chip % 2
            if s // 2 % 2:
                other = 1 - other
            twin = 1 - core if s % 2 else core
            p = (wrap(x + s // 4, nx) * 2 + other) * 2 + twin
            act(p, f_dev(p), s)

    barrier = pltpu.get_barrier_semaphore()

    def greet(dev):
        pl.semaphore_signal(barrier, inc=1, device_id=dev, device_id_type=MESH)

    t_peers(lambda slot, dev, number: greet(dev))
    f_peers(lambda slot, dev, number: greet(dev))
    pl.semaphore_wait(barrier, nt - 1 + nf - 1)

    order = [0]
    for d in range(1, ny // 2 + 1):
        order.append(d)
        if ny - d != d:
            order.append(ny - d)

    def y_dev(d):
        return (f, z * ny + (y + d) % ny)

    def k_copy(d):
        p = (y + d) % ny
        return copy(k_ref.at[0, :, chunk(p)], kpad.at[band_rows(y)], ks.at[d], kr.at[d], y_dev(d))

    def v_copy(d):
        p = (y + d) % ny
        return copy(v_ref.at[0, :, chunk(p)], vbuf.at[y], vs.at[d], vr.at[d], y_dev(d))

    def q_copy(d):
        p = (y + d) % ny
        return copy(q_ref.at[0, :, chunk(p)], qbuf.at[y], qs.at[d], qr.at[d], y_dev(d))

    others = order[1:]
    for d in others:
        k_copy(d).start()
    for d in others:
        q_copy(d).start()
    for d in others:
        v_copy(d).start()

    mine = pl.ds(pl.multiple_of(core * shard, 64), shard)
    holder = chip == y
    relay = (chip // 2 == y // 2) & (chip != y)
    leaf = chip // 2 != y // 2
    lines = range(1, nf // 4)

    def x_copy(src, d):
        return copy(src, rraw.at[mine], rs.at[d], rr.at[0], ((f + 4 * d) % nf, t))

    def mirror_copy():
        return copy(r_ref, rraw.at[mine], rs.at[0], rr.at[0], f_dev(f + 2 - 4 * (chip % 2)))

    def r_local():
        return pltpu.make_async_copy(r_ref, rraw.at[mine], local.at[3])

    @pl.when(holder)
    def _():
        mirror_copy().start()
        for d in lines:
            x_copy(r_ref, d).start()
        r_local().start()


    own_k.wait()
    for d in others:
        k_copy(d).wait_recv()
    for c in small:
        c.wait()
    gid = gid_ref[0]
    gid_y, gid_z = lax.rem(gid, ny), lax.div(gid, ny)

    def pick(parts, want):
        out = None
        for i, part in enumerate(parts):
            part = part.astype(F32) * jnp.where(want == i, 1.0, 0.0)
            out = part if out is None else out + part
        return out.astype(BF16)

    def z_dev(d):
        return (f, ((z + d) % nz) * ny + y)

    def z_copy(buf, ssem, rsem, d):
        return copy(buf.at[z], buf.at[z], ssem.at[d], rsem.at[d], z_dev(d))

    def k_ends():
        up = copy(kpad.at[pl.ds(rows, ROW)], kpad.at[pl.ds(0, ROW)], hks.at[0], hkr.at[0], z_dev(1))
        down = copy(kpad.at[pl.ds(ROW, ROW)], kpad.at[pl.ds(ROW + rows, ROW)], hks.at[1], hkr.at[1], z_dev(nz - 1))
        return up, down

    def v_ends():
        low, high = pl.ds(0, ROW), pl.ds(ROW, ROW)
        up = copy(vbuf.at[ny - 1, high], vend.at[low], hvs.at[0], hvr.at[0], z_dev(1))
        down = copy(vbuf.at[0, low], vend.at[high], hvs.at[1], hvr.at[1], z_dev(nz - 1))
        return up, down

    zk[z] = pick([kpad[ROW + b * BAND : ROW + (b + 1) * BAND, :] for b in range(ny)], gid_y)
    for d in range(1, nz):
        z_copy(zk, zks, zkr, d).start()
    for c in k_ends():
        c.start()

    q_gain = [qg_ref[pl.ds(y * hc + h, 1), :] for h in range(hc)]
    k_gain = [kg_ref[pl.ds(y * hc + h, 1), :] for h in range(hc)]
    knpad[:, :, HEAD:] = jnp.ones((hc, rows + 2 * ROW, HEAD), BF16)
    kng[:, :, HEAD:] = jnp.ones((hc, BAND, HEAD), BF16)

    def norm_rows(at, size):
        for h in range(hc):
            knpad[h, at, :HEAD] = normalize(kpad[at, h * HEAD : (h + 1) * HEAD], k_gain[h])

    def norm_band(b, carry):
        norm_rows(band_rows(b), BAND)
        return carry

    lax.fori_loop(0, ny, norm_band, 0)


    for d in range(1, nz):
        z_copy(zk, zks, zkr, d).wait_recv()
    for c in k_ends():
        c.wait_recv()
    norm_rows(pl.ds(0, ROW), ROW)
    norm_rows(pl.ds(ROW + rows, ROW), ROW)
    kg_raw = pick([zk[i] for i in range(nz)], gid_z)
    for h in range(hc):
        kng[h, :, :HEAD] = normalize(kg_raw[:, h * HEAD : (h + 1) * HEAD], k_gain[h])

    @pl.when(relay)
    def _():
        mirror_copy().wait_recv()
        for d in lines:
            x_copy(rraw.at[mine], d).start()

    ones16 = jnp.ones((16, BAND), BF16)
    lane = lax.broadcasted_iota(jnp.int32, (BAND, WIN), 1)

    def band(b):
        low = jnp.where((z == 0) & (b == 0), ROW, 0)
        high = jnp.where((z == nz - 1) & (b == ny - 1), ROW + BAND, WIN)
        usable = (lane >= low) & (lane < high)
        window = pl.ds(pl.multiple_of(b * BAND, BAND), WIN)
        for h in range(hc):
            qn = normalize(qbuf[b, :, h * HEAD : (h + 1) * HEAD], q_gain[h])
            qn_s[b, h] = qn
            near = dot(qn, knpad[h, window, :HEAD], NT) * SCALE
            far = dot(qn, kng[h, :, :HEAD], NT) * SCALE
            near = jnp.where(usable, near, -1e30)
            top = jnp.maximum(jnp.max(near, -1, keepdims=True), jnp.max(far, -1, keepdims=True))
            near = jnp.exp(near - top)
            far = jnp.exp(far - top)
            total = jnp.sum(near, -1, keepdims=True) + jnp.sum(far, -1, keepdims=True)
            inv = 1.0 / total
            near = (near * inv).astype(BF16)
            far = (far * inv).astype(BF16)
            att[b, h, :, :WIN] = near
            att[b, h, :, WIN:] = far
            w_s[b, h, :, :WIN] = dot(ones16, near, NN)[:8]
            w_s[b, h, :, WIN:] = dot(ones16, far, NN)[:8]

    own_q.wait()
    for d in order:
        if d:
            q_copy(ny - d).wait_recv()
        band((y + d) % ny)

    half = lax.broadcasted_iota(jnp.int32, (1, HEAD), 1) < ROW
    given = []
    zw[z] = jnp.zeros((8, HEAD), F32)
    for h in range(hc):
        parts = [jnp.zeros((1, HEAD), F32) for _ in range(ny + 1)]
        far = jnp.zeros((1, HEAD), F32)
        for b in range(ny):
            parts[b] = parts[b] + w_s[b, h, 0:1, :HEAD]
            parts[b + 1] = parts[b + 1] + w_s[b, h, 0:1, HEAD:WIN]
            far = far + w_s[b, h, 0:1, WIN:]
        given.append(parts)
        zw[z, h : h + 1, :] = far
        zw[z, hc + h : hc + h + 1, :] = jnp.where(half, parts[0], parts[ny])
    for d in range(1, nz):
        z_copy(zw, zws, zwr, d).start()

    @pl.when(holder)
    def _():
        r_local().wait()

    if nf > 4:

        @pl.when(leaf)
        def _():
            mirror_copy().wait_recv()

    def twin_copy(at):
        return copy(rraw.at[at], rraw.at[at], fs, fr, (f + 1 - 2 * core, t))

    twin_copy(mine).start()

    e_acc[...] = jnp.zeros_like(e_acc)
    eg_acc[...] = jnp.zeros_like(eg_acc)

    def pulled(b, carry):
        window = pl.ds(pl.multiple_of(b * BAND, BAND), WIN)
        for h in range(hc):
            near = att[b, h, :, :WIN]
            far = att[b, h, :, WIN:]
            kn = knpad[h, window, :]
            kg = kng[h]
            mean_key = dot(near, kn, NN) + dot(far, kg, NN)
            qn = qn_s[b, h]
            qk = qn.astype(F32) * (mean_key[:, :HEAD] / mean_key[:, HEAD:])
            qk_high = qk.astype(BF16)
            qk_low = (qk - qk_high.astype(F32)).astype(BF16)
            right = jnp.concatenate([qn, qk_high, qk_low], 1)
            got = dot(near, right, TN)
            e_acc[h, window, :] += (
                kn[:, :HEAD].astype(F32) * got[:, :HEAD] - got[:, HEAD : 2 * HEAD] - got[:, 2 * HEAD :]
            )
            got = dot(far, right, TN)
            eg_acc[h] += kg[:, :HEAD].astype(F32) * got[:, :HEAD] - got[:, HEAD : 2 * HEAD] - got[:, 2 * HEAD :]
        return carry

    def pull_bands(first, last):
        lax.fori_loop(min(first, ny), min(last, ny), pulled, 0)

    pull_bands(0, 4)

    other = pl.ds(pl.multiple_of((1 - core) * shard, 64), shard)
    twin_copy(other).wait_recv()
    rpad[:, CLASSES // HEAD * HEAD :] = jnp.zeros((width, PAD - CLASSES // HEAD * HEAD), BF16)
    rpad[:, :CLASSES] = rraw[...]

    for d in range(1, nz):
        z_copy(zw, zws, zwr, d).wait_recv()
    below = zw[lax.rem(z + nz - 1, nz)]
    above = zw[lax.rem(z + 1, nz)]
    all_far = zw[0]
    for i in range(1, nz):
        all_far = all_far + zw[i]
    weights = []
    for h in range(hc):
        parts = given[h]
        parts[0] = parts[0] + below[hc + h : hc + h + 1]
        parts[ny] = parts[ny] + above[hc + h : hc + h + 1]
        own = []
        for b in range(ny):
            tile = jnp.concatenate([parts[b][:, ROW:], parts[b + 1][:, :ROW]], 1)
            own.append(tile + all_far[h : h + 1] * jnp.where(gid == z * ny + b, 1.0, 0.0))
        weights.append(split3(jnp.concatenate(own, 1)))

    def v_head(h):
        return vbuf[:, :, h * HEAD : (h + 1) * HEAD].reshape(rows, HEAD)

    own_v.wait()
    for d in others:
        v_copy(d).wait_recv()
    pooled = [jnp.sum(dot(weights[h], v_head(h), NN), 0, keepdims=True) for h in range(hc)]
    pooled = jnp.concatenate(pooled, 1) * (1.0 / tokens)
    logits = row_dot(pooled, rpad[...], NN)
    for i in range(8):
        lbuf[t, i : i + 1, :] = logits[:, i * HEAD : (i + 1) * HEAD]

    def exchange(buf, me, peers, ssem, rsem):
        def out(dev, number):
            return copy(buf.at[me], buf.at[me], ssem.at[number], rsem.at[me], dev)

        def come(slot, dev):
            return copy(buf.at[slot], buf.at[slot], ssem.at[0], rsem.at[slot], dev)

        def start():
            peers(lambda slot, dev, number: out(dev, number).start())

        def wait():
            peers(lambda slot, dev, number: come(slot, dev).wait_recv(), True)

        def wait_sent():
            peers(lambda slot, dev, number: out(dev, number).wait_send(), True)

        return start, wait, wait_sent

    def total_of(buf, n):
        out = buf[0]
        for i in range(1, n):
            out = out + buf[i]
        return out

    l_start, l_wait, l_sent = exchange(lbuf, t, t_peers, lsem, lrem)
    p_start, p_wait, p_sent = exchange(pbuf, f, f_peers, psem, prem)
    w_start, w_wait, w_sent = exchange(wbuf, f, f_peers, wsem, wrem)
    t_start, t_wait, t_sent = exchange(tbuf, t, t_peers, tsem, trem)
    l_start()

    for c in v_ends():
        c.start()
    zv[z] = pick([vbuf[b] for b in range(ny)], gid_y)
    for d in range(1, nz):
        z_copy(zv, zvs, zvr, d).start()
    pull_bands(4, 7)

    l_wait()
    logits = total_of(lbuf, nt)
    place = lax.broadcasted_iota(jnp.int32, (8, HEAD), 0) * HEAD + lax.broadcasted_iota(jnp.int32, (8, HEAD), 1)
    valid = place < CLASSES
    logits = jnp.where(valid, logits, -jnp.inf)

    def all_sum(x):
        return jnp.sum(jnp.sum(x, 0, keepdims=True), 1, keepdims=True)

    top = jnp.max(jnp.max(logits, 0, keepdims=True), 1, keepdims=True)
    probs = jnp.exp(logits - top)
    probs = probs / all_sum(probs)
    pbuf[f] = probs
    p_start()

    pull_bands(7, ny)
    for d in range(1, nz):
        z_copy(zv, zvs, zvr, d).wait_recv()
    for c in v_ends():
        c.wait_recv()
    vg = pick([zv[i] for i in range(nz)], gid_z)
    e_bf[...] = e_acc[...].astype(BF16)
    ones_rows = jnp.ones((16, rows), BF16)
    for h in range(hc):
        cols = slice(h * HEAD, (h + 1) * HEAD)
        eg = eg_acc[h].astype(BF16)
        v = v_head(h)
        m = dot(v, e_bf[h, ROW : ROW + rows, :], TN) + dot(vg[:, cols], eg, TN)
        m = m + dot(vend[:ROW, cols], e_bf[h, :ROW, :], TN)
        m = m + dot(vend[ROW:, cols], e_bf[h, ROW + rows :, :], TN)
        middle = dot(v, ones_rows, (((0,), (1,)), ((), ())))[:, :1] * (1.0 / rows)
        total = jnp.sum(e_bf[h].astype(F32), 0, keepdims=True) + jnp.sum(eg.astype(F32), 0, keepdims=True)
        m = m - middle * total
        high = m.astype(BF16)
        pull[h, :, :HEAD] = high
        pull[h, :, HEAD:] = (m - high.astype(F32)).astype(BF16)

    p_wait()
    mean = total_of(pbuf, nf) * (1.0 / nf)
    log_mean = jnp.where(valid, jnp.log(mean), 0.0)
    entropy = -all_sum(jnp.where(valid, mean * log_mean, 0.0))
    ent_ref[...] = jnp.broadcast_to(entropy, ent_ref.shape)
    upstream = jnp.where(valid, -(log_mean + 1.0) * (1.0 / nf), 0.0)
    dlogits = probs * (upstream - all_sum(probs * upstream))
    dlogits = jnp.concatenate([dlogits[i : i + 1] for i in range(8)], 1)
    dpooled = row_dot(dlogits, rpad[...], NT) * (1.0 / tokens)
    wbuf[f] = jnp.zeros((8, HEAD), F32)
    for h in range(hc):
        cols = slice(h * HEAD, (h + 1) * HEAD)
        got = row_dot(dpooled[:, cols], pull[h], NN)
        wbuf[f, h : h + 1, :] = (got[:, :HEAD] + got[:, HEAD:]) * SCALE
    w_start()
    w_wait()
    tbuf[t] = total_of(wbuf, nf)
    t_start()

    for d in others:
        k_copy(d).wait_send()
        q_copy(d).wait_send()
        v_copy(d).wait_send()
    for d in range(1, nz):
        z_copy(zk, zks, zkr, d).wait_send()
        z_copy(zv, zvs, zvr, d).wait_send()
        z_copy(zw, zws, zwr, d).wait_send()
    for c in k_ends() + v_ends():
        c.wait_send()

    @pl.when(holder)
    def _():
        mirror_copy().wait_send()
        for d in lines:
            x_copy(r_ref, d).wait_send()

    @pl.when(relay)
    def _():
        for d in lines:
            x_copy(rraw.at[mine], d).wait_send()

    twin_copy(mine).wait_send()
    l_sent()
    p_sent()
    w_sent()
    t_sent()
    t_wait()
    for i in range(ny):
        got = None
        for j in range(nz):
            row = jnp.where(chip % 2 == 0, j, nz - 1 - j)
            part = tbuf[row * ny + i]
            got = part if got is None else got + part
        w_out[i * hc : (i + 1) * hc, :] = got[:hc]


def make_body(ny):
    def body(queries, keys, values, readout, global_block, q_gain, k_gain):
        nf, nt = lax.axis_size("fsdp"), lax.axis_size("tok")
        nz = nt // ny
        heads = q_gain.shape[0] // HEAD
        hc = heads // ny
        width = hc * HEAD
        rows = ny * BAND
        padded = rows + 2 * ROW
        tokens = nt * BAND
        dma = pltpu.SemaphoreType.DMA
        vmem = pltpu.VMEM
        scratch = [
            pltpu.SMEM((1,), jnp.int32),
            vmem((heads, HEAD), F32),
            vmem((heads, HEAD), F32),
            vmem((padded, width), BF16),
            vmem((ny, BAND, width), BF16),
            vmem((2 * ROW, width), BF16),
            vmem((ny, BAND, width), BF16),
            vmem((hc, padded, 2 * HEAD), BF16),
            vmem((hc, BAND, 2 * HEAD), BF16),
            vmem((nz, BAND, width), BF16),
            vmem((nz, BAND, width), BF16),
            vmem((nz, 8, HEAD), F32),
            vmem((width, CLASSES), BF16),
            vmem((width, PAD), BF16),
            vmem((ny, hc, BAND, SEEN), BF16),
            vmem((ny, hc, BAND, HEAD), BF16),
            vmem((ny, hc, 8, SEEN), F32),
            vmem((hc, padded, HEAD), F32),
            vmem((hc, BAND, HEAD), F32),
            vmem((hc, padded, HEAD), BF16),
            vmem((hc, HEAD, 2 * HEAD), BF16),
            vmem((nt, 8, HEAD), F32),
            vmem((nf, 8, HEAD), F32),
            vmem((nf, 8, HEAD), F32),
            vmem((nt, 8, HEAD), F32),
        ]
        scratch += [dma((ny,))] * 6 + [dma((7,))] + [dma((nz,))] * 4 + [dma((2,))] * 4 + [dma((nz,))] * 2
        scratch += [dma((nf // 4,)), dma((1,)), dma, dma]
        scratch += [dma((nt,))] * 2 + [dma((nf,))] * 4 + [dma((nt,))] * 2
        hbm = pl.BlockSpec(memory_space=pl.ANY)
        in_hbm = pl.BlockSpec(memory_space=pltpu.HBM)
        whole = pl.BlockSpec(memory_space=pltpu.VMEM)
        entropy, total = pl.pallas_call(
            functools.partial(kernel, ny, nz, nf, hc, tokens),
            out_shape=(
                jax.ShapeDtypeStruct((8, HEAD), F32),
                jax.ShapeDtypeStruct((heads, HEAD), F32),
            ),
            in_specs=[in_hbm, hbm, hbm, hbm, hbm, in_hbm, in_hbm],
            out_specs=(whole, whole),
            scratch_shapes=scratch,
            compiler_params=pltpu.CompilerParams(
                collective_id=0, has_side_effects=True, vmem_limit_bytes=60 * 2**20
            ),
            name="adapt",
        )(
            global_block,
            queries,
            keys,
            values,
            readout,
            q_gain.reshape(heads, HEAD),
            k_gain.reshape(heads, HEAD),
        )
        total = total.reshape(-1)
        return entropy[0, 0], total / q_gain, total / k_gain

    return body


def solution(mesh):
    in_specs = (
        P("fsdp", "tok", None),
        P("fsdp", "tok", None),
        P("fsdp", "tok", None),
        P("fsdp", None),
        P("fsdp"),
        P(),
        P(),
    )
    out_specs = (P(), P(), P())
    return jax.shard_map(make_body(Y), mesh=mesh, in_specs=in_specs, out_specs=out_specs, check_vma=False)
```
